32 devices in a mesh: rep: 4 (over y, x), fsdp: 8 (over z, core).
Axes of the slice: x: 2, y: 2, z: 4, core: 2. Of those that a mesh axis runs over, the one named last changes fastest.
Arguments:
- activations: bfloat16 [4, 6144, 6144], P('rep', 'fsdp'), may hold values from -6 to 6
- out_grads: bfloat16 [4, 6144, 512], P('rep', 'fsdp'), may hold values from -0.078125 to 0.078125
- momentum: float32 [4, 6144, 512], P('rep', 'fsdp'), may hold values from -6 to 6
- indices: int32 [4, 96, 8, 128], P('rep', 'fsdp'), may hold values from 0 to 4095, as said below
- counts: int32 [4], P('rep'), may hold values from 64 to 128, as said below
Outputs:
- new_momentum: float32 [4, 6144, 512], P('rep', 'fsdp')
- step_dir: float32 [6144, 512], P('fsdp')
The draws below stay inside these ranges and needn't reach their ends.
Inputs may be any that keep to these rules, and one draw needn't show every extreme that they name: `indices`: in each replica's list for one tile the 128 entries are distinct; only the first counts[r] slots of replica r are in use, the others hold further distinct positions that are not chosen. `counts`: the same count holds for every tile of one replica; some replica uses all 128 slots.
All inputs are finite; a program needn't handle non-finite values.
Results may differ from the reference program's by a relative error of at most 0.0003.
Values may be sent and summed in bfloat16 or wider, within the bound.
A program may use at most 192 MiB of HBM per device.

```python
import math
import jax
import jax.numpy as jnp
from jax import lax

D = 6144
LAT = 512
CH = 64
SLOTS = 128
REPS = 4
TOKENS = 6144


def draw_counts(key, part):
    key = jax.random.fold_in(key, 11)
    first, second = jax.random.split(key)
    drawn = jax.random.randint(first, (REPS,), SLOTS // 2, SLOTS + 1, dtype=jnp.int32)
    chosen = jax.random.randint(second, (), 0, REPS, dtype=jnp.int32)
    return jnp.where(jnp.arange(REPS, dtype=jnp.int32) == chosen, SLOTS, drawn).astype(jnp.int32)


def draw_indices(key, part):
    key = jax.random.fold_in(key, 23)
    tile_count = REPS * (D // CH) * (LAT // CH)
    flat_size = CH * CH
    scores = jax.random.randint(key, (tile_count, flat_size), 0, 262144, dtype=jnp.int32) * flat_size
    scores = scores + jnp.arange(flat_size, dtype=jnp.int32)[None, :]
    order = jnp.argsort(scores, axis=1, stable=True).astype(jnp.int32)
    return order[:, :SLOTS].reshape(REPS, D // CH, LAT // CH, SLOTS)


def strengthened(entries, key, source, target, parts, factor):
    owner, partner = [(jnp.arange(entries.shape[position]) // (entries.shape[position] // parts)).reshape([-1 if axis == position else 1 for axis in range(entries.ndim)]) for position in (source, target)]
    chosen = jax.random.permutation(key, parts)[partner]
    strong = (owner == chosen) | (owner == (partner + parts // 2) % parts)
    return jnp.where(strong, factor * entries, entries)


def shard_levels(own_key, shape, pieces, smallest, largest):
    loudness, own = 1.0, jax.random.fold_in(own_key, 6)
    for dim, blocks in pieces:
        heights = jnp.exp(jax.random.uniform(jax.random.fold_in(own, dim), (blocks,), jnp.float32, smallest / len(pieces), largest / len(pieces)))
        loudness = loudness * jnp.repeat(heights, shape[dim] // blocks).reshape([-1 if axis == dim else 1 for axis in range(len(shape))])
    return loudness


def centred(stream_key, dims, spread, bound, shards=(), kind=jnp.bfloat16):
    values = jax.random.normal(stream_key, dims, jnp.float32) * spread
    if len(shards) > 0:
        values = shard_levels(stream_key, dims, shards, -0.22, 0.18) * values
    return jnp.clip(values, min=-bound, max=bound).astype(kind)


def gaussian_with(rng, dims, spread, reach, pieces, heavy, kind=jnp.bfloat16):
    values = spread * jax.random.normal(rng, dims, jnp.float32)
    if pieces:
        values = values * shard_levels(rng, dims, pieces, -0.22, 0.18)
    return jnp.clip(strengthened(values, jax.random.fold_in(rng, 3), *heavy), -reach, reach).astype(kind)


def setup_inputs(seed: int = 0) -> dict:
    seeds = jax.random.split(jax.random.key(seed), 6)
    return {
        "activations": gaussian_with(seeds[0], (REPS, TOKENS, D), 1.0, 6.0, ((0, 4), (1, 8)), (1, 2, 8, 2.0)),
        "out_grads": centred(seeds[1], (REPS, TOKENS, LAT), TOKENS ** -0.5, 0.078125, ((0, 4), (1, 8))),
        "momentum": centred(seeds[2], (REPS, D, LAT), 1.0, 6.0, ((0, 4), (1, 8)), jnp.float32),
        "indices": draw_indices(jax.random.fold_in(seeds[5], 71), 0),
        "counts": draw_counts(jax.random.fold_in(seeds[5], 71), 0),
    }


def cosine_table(size):
    freq = lax.broadcasted_iota(jnp.int32, (size, size), 0).astype(jnp.float32)
    place = lax.broadcasted_iota(jnp.int32, (size, size), 1).astype(jnp.float32)
    table = jnp.cos(math.pi * (2.0 * place + 1.0) * freq / (2.0 * size)) * math.sqrt(2.0 / size)
    return jnp.where(freq < 0.5, table * math.sqrt(0.5), table)

def forward_tiles(field, table):
    height, breadth = field.shape
    side = table.shape[0]
    blocks = field.reshape(height // side, side, breadth // side, side)
    result = jnp.einsum('ka,iajb,lb->ijkl', table, blocks, table, precision=lax.Precision.HIGHEST)
    return result.reshape(height // side, breadth // side, side * side)

def inverse_tiles(values, table):
    tile_rows, tile_cols, flat_size = values.shape
    side = table.shape[0]
    grid = values.reshape(tile_rows, tile_cols, side, side)
    blocks = jnp.einsum('ka,ijkl,lb->iajb', table, grid, table, precision=lax.Precision.HIGHEST)
    return blocks.reshape(tile_rows * side, tile_cols * side)

def scatter_slots(values, places, flat_size):
    tile_rows, tile_cols, width_slots = values.shape
    tile_count = tile_rows * tile_cols
    tile_ids = jnp.broadcast_to(jnp.arange(tile_count, dtype=jnp.int32)[:, None], (tile_count, width_slots))
    dense = jnp.zeros((tile_count, flat_size), values.dtype)
    dense = dense.at[tile_ids, places.reshape(tile_count, width_slots).astype(jnp.int32)].add(values.reshape(tile_count, width_slots))
    return dense.reshape(tile_rows, tile_cols, flat_size)

def reference(activations, out_grads, momentum, indices, counts):
    table = cosine_table(CH)

    def one_replica(items):
        inputs, grads, moment_old, places, count = items
        gradient = jnp.einsum('td,tc->dc', inputs.astype(jnp.float32), grads.astype(jnp.float32), precision=lax.Precision.HIGHEST)
        moment = 0.9 * moment_old + gradient
        coefficients = forward_tiles(moment, table)
        picked = jnp.take_along_axis(coefficients, places, axis=2)
        live = jnp.arange(SLOTS, dtype=jnp.int32) < count
        picked = jnp.where(live, picked, jnp.zeros_like(picked))
        sparse = scatter_slots(picked, places, CH * CH)
        return (moment - inverse_tiles(sparse, table), sparse)
    new_momentum, sparse = lax.map(one_replica, (activations, out_grads, momentum, indices, counts))
    total = lax.optimization_barrier(jnp.sum(sparse, axis=0))
    decoded = inverse_tiles(total, table)
    step_dir = decoded * lax.rsqrt(decoded * decoded + 0.04)
    return (new_momentum, step_dir)
```

```python
import functools
import math

import jax
import jax.numpy as jnp
import numpy as np
from jax import lax
from jax.experimental import pallas as pl
from jax.experimental.pallas import tpu as pltpu
from jax.sharding import PartitionSpec as P
import ml_dtypes

CH = 64
MESH = pl.DeviceIdType.MESH
LEVELS = 32000.0


def cosine_tables():
    freq = np.arange(CH, dtype=np.float64)[:, None]
    place = np.arange(CH, dtype=np.float64)[None, :]
    table = np.cos(math.pi * (2 * place + 1) * freq / (2 * CH)) * math.sqrt(2.0 / CH)
    table[0] *= math.sqrt(0.5)

    def pieces(matrix):
        whole = matrix.astype(np.float32)
        head = whole.astype(ml_dtypes.bfloat16)
        tail = (whole - head.astype(np.float32)).astype(ml_dtypes.bfloat16)
        return [head, tail]

    left = np.kron(np.eye(2), table)
    right = np.kron(np.eye(4), table)
    return (
        np.stack(pieces(left) + pieces(left.T)),
        np.stack(pieces(right.T) + pieces(right)),
    )


def split(value):
    head = value.astype(jnp.bfloat16)
    return head, (value - head.astype(jnp.float32)).astype(jnp.bfloat16)


def dot(a, b, contract=((1,), (0,))):
    return lax.dot_general(a, b, (contract, ((), ())), preferred_element_type=jnp.float32)


def transform(field, left, right, way):
    lh, ll = left[2 * way], left[2 * way + 1]
    rh, rl = right[2 * way], right[2 * way + 1]
    parts = []
    for start in range(0, field.shape[1], 256):
        fh, fl = split(field[:, start : start + 256])
        parts.append(dot(fh, rh) + (dot(fh, rl) + dot(fl, rh)))
    yh, yl = split(jnp.concatenate(parts, axis=1))
    return dot(lh, yh) + (dot(lh, yl) + dot(ll, yh))


def pair_rows(rows, pair):
    a = rows[2 * pair : 2 * pair + 1, :]
    b = rows[2 * pair + 1 : 2 * pair + 2, :]
    return a, b


def row_codes(rows, pair):
    a, b = pair_rows(rows, pair)
    return jnp.concatenate([a >> 6, b >> 6], axis=1)


def column_hot(rows, pair):
    a, b = pair_rows(rows, pair)
    codes = jnp.concatenate([a & 63, (b & 63) + 64], axis=1)
    spots = lax.broadcasted_iota(jnp.int32, (2 * CH, codes.shape[1]), 0)
    return jnp.where(spots == codes, 1.0, 0.0).astype(jnp.bfloat16)


def kernel(
    sizes,
    counts_ref, act_hbm, grad_hbm, mom_hbm, places_ref, left_ref, right_ref,
    new_ref, step_ref,
    own_act, sib_act, own_grad, sib_grad, mom, acc, coded, scales, in_coded, in_scales,
    lists, values, mask, cols_hot, total,
    act_sem, sib_send, sib_recv, misc_sem, out_send, out_recv, rep_send, rep_recv,
):
    lines, reps, rows, chunk, pieces, width, tokens = sizes
    tile_rows, pairs = rows // CH, width // CH // 2
    f = lax.axis_index("fsdp")
    rep = lax.axis_index("rep")
    z, core = f // 2, f % 2
    sibling = {"fsdp": 2 * z + 1 - core}

    def along(step):
        return {"fsdp": 2 * (z + step) + core}

    barrier = pltpu.get_barrier_semaphore()
    pl.semaphore_signal(barrier, inc=1, device_id=sibling, device_id_type=MESH)

    @pl.when(z > 0)
    def _():
        pl.semaphore_signal(barrier, inc=1, device_id=along(-1), device_id_type=MESH)

    @pl.when(z < lines - 1)
    def _():
        pl.semaphore_signal(barrier, inc=1, device_id=along(1), device_id_type=MESH)

    for o in range(1, reps):
        pl.semaphore_signal(
            barrier, inc=1, device_id={"rep": lax.rem(rep + o, reps)}, device_id_type=MESH
        )

    def source(q, lane):
        start = (2 * (q // pieces) + lane) * rows + (q % pieces) * chunk
        return act_hbm.at[:, pl.ds(pl.multiple_of(start, 128), chunk)]

    def own_copy(q):
        return pltpu.make_async_copy(source(q, core), own_act.at[q], act_sem.at[q])

    def sib_copy(q):
        return pltpu.make_async_remote_copy(
            src_ref=source(q, 1 - core), dst_ref=sib_act.at[q],
            send_sem=sib_send.at[q], recv_sem=sib_recv.at[q],
            device_id=sibling, device_id_type=MESH,
        )

    grad_own = pltpu.make_async_copy(grad_hbm, own_grad, misc_sem.at[0])
    mom_own = pltpu.make_async_copy(mom_hbm, mom, misc_sem.at[1])
    grad_sib = pltpu.make_async_remote_copy(
        src_ref=grad_hbm, dst_ref=sib_grad, send_sem=misc_sem.at[2], recv_sem=misc_sem.at[3],
        device_id=sibling, device_id_type=MESH,
    )
    grad_own.start()
    neighbours = 1 + jnp.where(z > 0, 1, 0) + jnp.where(z < lines - 1, 1, 0) + (reps - 1)
    pl.semaphore_wait(barrier, neighbours)
    grad_sib.start()

    def each(k, right, left):
        far, piece = k // pieces, k % pieces

        @pl.when(lines - 1 - far > z)
        def _():
            right((lines - 1 - far) * pieces + piece)

        @pl.when(far < z)
        def _():
            left(far * pieces + piece)

    steps = (lines - 1) * pieces

    def fetch(q):
        own_copy(q).start()
        sib_copy(q).start()

    def fetch_step(k, carry):
        each(k, fetch, fetch)
        return carry

    lax.fori_loop(0, steps, fetch_step, 0)
    for piece in range(pieces):
        fetch(z * pieces + piece)
    mom_own.start()

    slot = lax.broadcasted_iota(jnp.int32, places_ref.shape, 2)
    lists[rep] = jnp.where(slot < counts_ref[0], places_ref[...], -1)

    def list_copy(o, buffer, kind):
        return pltpu.make_async_remote_copy(
            src_ref=buffer.at[rep], dst_ref=buffer.at[rep],
            send_sem=rep_send.at[kind, o], recv_sem=rep_recv.at[kind, o],
            device_id={"rep": lax.rem(rep + o, reps)}, device_id_type=MESH,
        )

    for o in range(1, reps):
        list_copy(o, lists, 0).start()

    grad_own.wait()
    grad_sib.wait()

    def partial(q):
        own_copy(q).wait()
        sib_copy(q).wait_recv()
        over = ((0,), (0,))
        acc[...] = dot(own_act[q], own_grad[...], over) + dot(sib_act[q], sib_grad[...], over)

    def chunk_copies(q, way, step):
        return [
            pltpu.make_async_remote_copy(
                src_ref=src.at[q], dst_ref=dst.at[way, q],
                send_sem=out_send.at[kind, q], recv_sem=out_recv.at[kind, way, q],
                device_id=along(step), device_id_type=MESH,
            )
            for kind, (src, dst) in enumerate(((coded, in_coded), (scales, in_scales)))
        ]

    def add_arrived(q, way, step):
        for copy in chunk_copies(q, way, step):
            copy.wait_recv()
        acc[...] += in_coded[way, q].astype(jnp.int32).astype(jnp.float32) * in_scales[way, q]

    def pass_on(q, way, step):
        value = acc[...]
        top = jnp.maximum(jnp.max(jnp.abs(value), axis=0, keepdims=True), 1e-30)
        scales[q] = top * (1.0 / LEVELS)
        coded[q] = jnp.round(value * (LEVELS / top)).astype(jnp.int32).astype(jnp.int16)
        for copy in chunk_copies(q, way, step):
            copy.start()

    def right(q):
        partial(q)

        @pl.when(z > 0)
        def _():
            add_arrived(q, 0, 1)

        pass_on(q, 0, 1)

    def left(q):
        partial(q)

        @pl.when(z < lines - 1)
        def _():
            add_arrived(q, 1, -1)

        pass_on(q, 1, -1)

    def line_step(k, carry):
        each(k, right, left)
        return carry

    lax.fori_loop(0, 1, line_step, 0)

    def mask_step(i, carry):
        codes = lists[rep, i]
        for pair in range(pairs):
            row = row_codes(codes, pair)
            spots = lax.broadcasted_iota(jnp.int32, (CH, row.shape[1]), 0)
            hot = jnp.where(spots == row, 1.0, 0.0).astype(jnp.bfloat16)
            cols = column_hot(codes, pair)
            mask[pl.ds(pl.multiple_of(i * CH, CH), CH), 2 * CH * pair : 2 * CH * (pair + 1)] = (
                dot(hot, cols, ((1,), (1,)))
            )
        return carry

    lax.fori_loop(0, tile_rows, mask_step, 0)
    lax.fori_loop(1, steps, line_step, 0)

    for o in range(1, reps):
        list_copy(o, lists, 0).wait()

    def hot_step(n, carry):
        codes = lists[n // tile_rows, n % tile_rows]
        for pair in range(pairs):
            cols_hot[n, pair] = column_hot(codes, pair)
        return carry

    lax.fori_loop(0, reps * tile_rows, hot_step, 0)

    mom_own.wait()
    group = 2 * CH

    for piece in range(pieces):
        q = z * pieces + piece
        partial(q)

        @pl.when(z > 0)
        def _():
            add_arrived(q, 0, 1)

        @pl.when(z < lines - 1)
        def _():
            add_arrived(q, 1, -1)

        for part in range(chunk // group):
            start = piece * chunk + part * group
            here = slice(start, start + group)
            moment = 0.9 * mom[here, :] + acc[part * group : (part + 1) * group, :]
            coefficients = transform(moment, left_ref, right_ref, 0)
            chosen = jnp.where(mask[here, :] > 0.5, coefficients, 0.0)
            new_ref[here, :] = moment - transform(chosen, left_ref, right_ref, 1)
            head, tail = split(coefficients)
            for half in range(2):
                i = start // CH + half
                codes = lists[rep, i]
                picks = []
                for pair in range(pairs):
                    at = (slice(half * CH, (half + 1) * CH), slice(2 * CH * pair, 2 * CH * (pair + 1)))
                    cols = cols_hot[rep * tile_rows + i, pair]
                    found = dot(jnp.concatenate([head[at], tail[at]], axis=0), cols)
                    found = found[:CH] + found[CH:]
                    row = row_codes(codes, pair)
                    spots = lax.broadcasted_iota(jnp.int32, found.shape, 0)
                    pick = jnp.sum(jnp.where(spots == row, found, 0.0), axis=0, keepdims=True)
                    picks += [pick[:, : pick.shape[1] // 2], pick[:, pick.shape[1] // 2 :]]
                values[rep, i] = jnp.concatenate(picks, axis=0)

    for o in range(1, reps):
        list_copy(o, values, 1).start()
    for o in range(1, reps):
        list_copy(o, values, 1).wait()

    def total_step(i, carry):
        for pair in range(pairs):
            result = jnp.zeros((2 * CH, 2 * CH), jnp.float32)
            for r in range(reps):
                row = row_codes(lists[r, i], pair)
                a, b = pair_rows(values[r, i], pair)
                head, tail = split(jnp.concatenate([a, b], axis=1))
                spots = lax.broadcasted_iota(jnp.int32, (CH, row.shape[1]), 0)
                hit = spots == row
                both = jnp.concatenate(
                    [
                        jnp.where(hit, head.astype(jnp.float32), 0.0),
                        jnp.where(hit, tail.astype(jnp.float32), 0.0),
                    ],
                    axis=0,
                ).astype(jnp.bfloat16)
                result += dot(both, cols_hot[r * tile_rows + i, pair], ((1,), (1,)))
            total[pl.ds(pl.multiple_of(i * CH, CH), CH), 2 * CH * pair : 2 * CH * (pair + 1)] = (
                result[:CH] + result[CH:]
            )
        return carry

    lax.fori_loop(0, tile_rows, total_step, 0)
    for start in range(0, rows, group):
        decoded = transform(total[start : start + group, :], left_ref, right_ref, 1)
        step_ref[start : start + group, :] = decoded * lax.rsqrt(decoded * decoded + 0.04)

    def sent(way, step):
        def wait(q):
            for copy in chunk_copies(q, way, step):
                copy.wait_send()
            sib_copy(q).wait_send()

        return wait

    def sent_step(k, carry):
        each(k, sent(0, 1), sent(1, -1))
        return carry

    lax.fori_loop(0, steps, sent_step, 0)
    for piece in range(pieces):
        sib_copy(z * pieces + piece).wait_send()


def body(lines, reps, activations, out_grads, momentum, indices, counts):
    inputs, grads, moment, places = activations[0], out_grads[0], momentum[0], indices[0]
    tokens, model = inputs.shape
    owned, width = moment.shape
    tile_cols, slots = places.shape[1:]
    fill = -owned % (2 * CH)
    rows = owned + fill
    if fill:
        inputs = inputs.reshape(tokens, 2 * lines, owned)
        inputs = jnp.pad(inputs, ((0, 0), (0, 0), (0, fill))).reshape(tokens, 2 * lines * rows)
        moment = jnp.pad(moment, ((0, fill), (0, 0)))
        places = jnp.pad(places, ((0, fill // CH), (0, 0), (0, 0)), constant_values=-1)
    tile_rows = rows // CH
    pieces = 3 if rows % (6 * CH) == 0 else rows // (2 * CH)
    chunk = rows // pieces
    count = lines * pieces
    left, right = cosine_tables()
    sizes = (lines, reps, rows, chunk, pieces, width, tokens)
    vmem = pl.BlockSpec(memory_space=pltpu.VMEM)
    hbm = pl.BlockSpec(memory_space=pl.ANY)
    dma = pltpu.SemaphoreType.DMA
    new_moment, step_dir = pl.pallas_call(
        functools.partial(kernel, sizes),
        out_shape=(
            jax.ShapeDtypeStruct((rows, width), jnp.float32),
            jax.ShapeDtypeStruct((rows, width), jnp.float32),
        ),
        in_specs=[pl.BlockSpec(memory_space=pltpu.SMEM), hbm, hbm, hbm, vmem, vmem, vmem],
        out_specs=(vmem, vmem),
        scratch_shapes=[
            pltpu.VMEM((count, tokens, chunk), jnp.bfloat16),
            pltpu.VMEM((count, tokens, chunk), jnp.bfloat16),
            pltpu.VMEM((tokens, width), jnp.bfloat16),
            pltpu.VMEM((tokens, width), jnp.bfloat16),
            pltpu.VMEM((rows, width), jnp.float32),
            pltpu.VMEM((chunk, width), jnp.float32),
            pltpu.VMEM((count, chunk, width), jnp.int16),
            pltpu.VMEM((count, 1, width), jnp.float32),
            pltpu.VMEM((2, count, chunk, width), jnp.int16),
            pltpu.VMEM((2, count, 1, width), jnp.float32),
            pltpu.VMEM((reps, tile_rows, tile_cols, slots), jnp.int32),
            pltpu.VMEM((reps, tile_rows, tile_cols, slots), jnp.float32),
            pltpu.VMEM((rows, width), jnp.float32),
            pltpu.VMEM((reps * tile_rows, tile_cols // 2, 2 * CH, 2 * slots), jnp.bfloat16),
            pltpu.VMEM((rows, width), jnp.float32),
            dma((count,)),
            dma((count,)),
            dma((count,)),
            dma((4,)),
            dma((2, count)),
            dma((2, 2, count)),
            dma((2, reps)),
            dma((2, reps)),
        ],
        compiler_params=pltpu.CompilerParams(
            collective_id=0, has_side_effects=True, vmem_limit_bytes=60 * 1024 * 1024
        ),
        cost_estimate=pl.CostEstimate(
            flops=2 * tokens * model * width, bytes_accessed=2 * tokens * model, transcendentals=0
        ),
    )(counts, inputs, grads, moment, places, jnp.asarray(left), jnp.asarray(right))
    return (new_moment[None, :owned], step_dir[:owned])


def solution(mesh):
    lines, reps = mesh.shape["fsdp"] // 2, mesh.shape["rep"]
    placed = (
        P("rep", "fsdp", None),
        P("rep", "fsdp", None),
        P("rep", "fsdp", None),
        P("rep", "fsdp", None, None),
        P("rep"),
    )
    return jax.shard_map(
        functools.partial(body, lines, reps),
        mesh=mesh,
        in_specs=placed,
        out_specs=(P("rep", "fsdp", None), P("fsdp", None)),
        check_vma=False,
    )
```

```python
import functools
import math

import jax
import jax.numpy as jnp
import numpy as np
from jax import lax
from jax.experimental import pallas as pl
from jax.experimental.pallas import tpu as pltpu
from jax.sharding import PartitionSpec as P
import ml_dtypes

CH = 64
MESH = pl.DeviceIdType.MESH
LEVELS = 32000.0


def cosine_tables():
    freq = np.arange(CH, dtype=np.float64)[:, None]
    place = np.arange(CH, dtype=np.float64)[None, :]
    table = np.cos(math.pi * (2 * place + 1) * freq / (2 * CH)) * math.sqrt(2.0 / CH)
    table[0] *= math.sqrt(0.5)
    whole = np.kron(np.eye(4), table).astype(np.float32)
    head = whole.astype(ml_dtypes.bfloat16)
    tail = (whole - head.astype(np.float32)).astype(ml_dtypes.bfloat16)
    return np.stack([head.T, tail.T, head, tail])


def split(value):
    head = value.astype(jnp.bfloat16)
    return head, (value - head.astype(jnp.float32)).astype(jnp.bfloat16)


def dot(a, b, contract=((1,), (0,))):
    return lax.dot_general(a, b, (contract, ((), ())), preferred_element_type=jnp.float32)


def transform(field, tables, way):
    height, width = field.shape
    rh, rl = tables[2 * way], tables[2 * way + 1]
    other = 2 - 2 * way
    lh, ll = tables[other, :height, :height], tables[other + 1, :height, :height]
    stack = jnp.concatenate([lh, ll], axis=0)
    parts = []
    for start in range(0, width, 256):
        fh, fl = split(field[:, start : start + 256])
        both = dot(jnp.concatenate([fh, fl], axis=0), rh)
        yh, yl = split(both[:height] + (dot(fh, rl) + both[height:]))
        both = dot(stack, yh)
        parts.append(both[:height] + (dot(lh, yl) + both[height:]))
    return jnp.concatenate(parts, axis=1)


def pair_rows(rows, pair):
    a = rows[2 * pair : 2 * pair + 1, :]
    b = rows[2 * pair + 1 : 2 * pair + 2, :]
    return a, b


def row_codes(rows, pair):
    a, b = pair_rows(rows, pair)
    return jnp.concatenate([a >> 6, b >> 6], axis=1)


def column_hot(rows, pair):
    a, b = pair_rows(rows, pair)
    codes = jnp.concatenate([a & 63, (b & 63) + 64], axis=1)
    spots = lax.broadcasted_iota(jnp.int32, (2 * CH, codes.shape[1]), 0)
    return jnp.where(spots == codes, 1.0, 0.0).astype(jnp.bfloat16)


def kernel(
    sizes,
    counts_ref, act_hbm, grad_hbm, mom_hbm, places_ref, tables,
    new_hbm, dec_hbm,
    own_act, sib_act, own_grad, sib_grad, flipped, mom, acc, coded, scales, in_coded, in_scales,
    lists, values, mask, cols_hot, total, decoded,
    act_sem, sib_send, sib_recv, misc_sem, out_send, out_recv, rep_send, rep_recv, res_sem,
):
    lines, reps, rows, chunk, pieces, width, tokens = sizes
    pairs = width // CH // 2
    tile_rows = rows // CH
    piece_tiles = chunk // CH
    f = lax.axis_index("fsdp")
    rep = lax.axis_index("rep")
    z, core = f // 2, f % 2
    sibling = {"fsdp": 2 * z + 1 - core}

    def along(step):
        return {"fsdp": 2 * (z + step) + core}

    grad_own = pltpu.make_async_copy(grad_hbm, own_grad, misc_sem.at[0])
    mom_own = pltpu.make_async_copy(mom_hbm, mom, misc_sem.at[1])
    grad_own.start()

    barrier = pltpu.get_barrier_semaphore()
    pl.semaphore_signal(barrier, inc=1, device_id=sibling, device_id_type=MESH)

    @pl.when(z > 0)
    def _():
        pl.semaphore_signal(barrier, inc=1, device_id=along(-1), device_id_type=MESH)

    @pl.when(z < lines - 1)
    def _():
        pl.semaphore_signal(barrier, inc=1, device_id=along(1), device_id_type=MESH)

    for o in range(1, reps):
        pl.semaphore_signal(
            barrier, inc=1, device_id={"rep": lax.rem(rep + o, reps)}, device_id_type=MESH
        )

    used = lax.broadcasted_iota(jnp.int32, places_ref.shape[1:], 1) < counts_ref[...]
    for i in range(tile_rows):
        lists[rep, i] = jnp.where(used, places_ref[i], -1)

    def source(q, lane):
        start = (2 * (q // pieces) + lane) * rows + (q % pieces) * chunk
        return act_hbm.at[:, pl.ds(pl.multiple_of(start, 128), chunk)]

    def own_copy(q):
        return pltpu.make_async_copy(source(q, core), own_act.at[q], act_sem.at[q])

    def sib_copy(q):
        return pltpu.make_async_remote_copy(
            src_ref=source(q, 1 - core), dst_ref=sib_act.at[q],
            send_sem=sib_send.at[q], recv_sem=sib_recv.at[q],
            device_id=sibling, device_id_type=MESH,
        )

    grad_sib = pltpu.make_async_remote_copy(
        src_ref=grad_hbm, dst_ref=sib_grad, send_sem=misc_sem.at[2], recv_sem=misc_sem.at[3],
        device_id=sibling, device_id_type=MESH,
    )

    steps = (lines - 1) * pieces
    plain = (lines - 3) * pieces

    def owner(k):
        later = k - plain
        block = jnp.where(later < 0, lines - 1 - k // pieces, 2 - later % 2)
        piece = jnp.where(later < 0, k % pieces, later // 2)
        return block, piece

    def each(k, right, left):
        block, piece = owner(k)

        @pl.when(block > z)
        def _():
            right(block * pieces + piece)

        @pl.when(lines - 1 - block < z)
        def _():
            left((lines - 1 - block) * pieces + piece)

    def fetch(q):
        own_copy(q).start()
        sib_copy(q).start()

    neighbours = 1 + jnp.where(z > 0, 1, 0) + jnp.where(z < lines - 1, 1, 0) + (reps - 1)
    pl.semaphore_wait(barrier, neighbours)
    grad_sib.start()
    each(0, fetch, fetch)

    def list_copy(o):
        return pltpu.make_async_remote_copy(
            src_ref=lists.at[rep], dst_ref=lists.at[rep],
            send_sem=rep_send.at[pieces, o], recv_sem=rep_recv.at[pieces, o],
            device_id={"rep": lax.rem(rep + o, reps)}, device_id_type=MESH,
        )

    def value_copy(o, m):
        part = values.at[rep, pl.ds(m * piece_tiles, piece_tiles)]
        return pltpu.make_async_remote_copy(
            src_ref=part, dst_ref=part,
            send_sem=rep_send.at[m, o], recv_sem=rep_recv.at[m, o],
            device_id={"rep": lax.rem(rep + o, reps)}, device_id_type=MESH,
        )

    grad_own.wait()
    flipped[0] = own_grad[...].T
    grad_sib.wait()
    flipped[1] = sib_grad[...].T
    for k in range(1, min(2, steps)):
        each(k, fetch, fetch)
    for o in range(1, reps):
        list_copy(o).start()

    def partial(q):
        own_copy(q).wait()
        sib_copy(q).wait_recv()
        acc[...] = dot(flipped[0], own_act[q]) + dot(flipped[1], sib_act[q])

    def chunk_copies(q, way, step):
        return [
            pltpu.make_async_remote_copy(
                src_ref=src.at[q], dst_ref=dst.at[way, q],
                send_sem=out_send.at[kind, q], recv_sem=out_recv.at[kind, way, q],
                device_id=along(step), device_id_type=MESH,
            )
            for kind, (src, dst) in enumerate(((coded, in_coded), (scales, in_scales)))
        ]

    def add_arrived(q, way, step):
        for copy in chunk_copies(q, way, step):
            copy.wait_recv()
        acc[...] += in_coded[way, q].astype(jnp.int32).astype(jnp.float32) * in_scales[way, q]

    def pass_on(q, way, step):
        value = acc[...]
        top = jnp.maximum(jnp.max(jnp.abs(value), axis=0, keepdims=True), 1e-30)
        scales[q] = top * (1.0 / LEVELS)
        coded[q] = jnp.round(value * (LEVELS / top)).astype(jnp.int32).astype(jnp.int16)
        for copy in chunk_copies(q, way, step):
            copy.start()

    def right(q):
        partial(q)

        @pl.when(z > 0)
        def _():
            add_arrived(q, 0, 1)

        pass_on(q, 0, 1)

    def left(q):
        partial(q)

        @pl.when(z < lines - 1)
        def _():
            add_arrived(q, 1, -1)

        pass_on(q, 1, -1)

    def sent(way, step):
        def wait(q):
            for copy in chunk_copies(q, way, step):
                copy.wait_send()

        return wait

    def line_step(k, carry):
        @pl.when(k >= 2)
        def _():
            each(k - 2, sent(0, 1), sent(1, -1))

        @pl.when(k + 2 < steps)
        def _():
            each(k + 2, fetch, fetch)

        @pl.when(k < pieces)
        def _():
            fetch(z * pieces + k)

        each(k, right, left)
        return carry

    def mask_step(i, carry):
        codes = lists[rep, i]
        for pair in range(pairs):
            row = row_codes(codes, pair)
            spots = lax.broadcasted_iota(jnp.int32, (CH, row.shape[1]), 0)
            hot = jnp.where(spots == row, 1.0, 0.0).astype(jnp.bfloat16)
            cols = column_hot(codes, pair)
            mask[pl.ds(pl.multiple_of(i * CH, CH), CH), 2 * CH * pair : 2 * CH * (pair + 1)] = (
                dot(hot, cols, ((1,), (1,)))
            )
        return carry

    def hot_step(n, carry):
        codes = lists[n // tile_rows, n % tile_rows]
        for pair in range(pairs):
            cols_hot[n, pair] = column_hot(codes, pair)
        return carry

    def prepare():
        mom_own.start()
        lax.fori_loop(0, tile_rows, mask_step, 0)
        for o in range(1, reps):
            list_copy(o).wait()
        lax.fori_loop(0, reps * tile_rows, hot_step, 0)
        mom_own.wait()

    middle = (z > 0) & (z < lines - 1)

    @pl.when(middle)
    def _():
        prepare()

    line_step(0, 0)

    @pl.when(jnp.logical_not(middle))
    def _():
        prepare()

    lax.fori_loop(1, max(plain, 1), line_step, 0)

    def decode(m):
        for o in range(1, reps):
            value_copy(o, m).wait()

        def tile_step(h, carry):
            i = m * piece_tiles + h
            for pair in range(pairs):
                result = jnp.zeros((2 * CH, 2 * CH), jnp.float32)
                for r in range(reps):
                    row = row_codes(lists[r, i], pair)
                    a, b = pair_rows(values[r, i], pair)
                    head, tail = split(jnp.concatenate([a, b], axis=1))
                    spots = lax.broadcasted_iota(jnp.int32, (CH, row.shape[1]), 0)
                    hit = spots == row
                    both = jnp.concatenate(
                        [
                            jnp.where(hit, head.astype(jnp.float32), 0.0),
                            jnp.where(hit, tail.astype(jnp.float32), 0.0),
                        ],
                        axis=0,
                    ).astype(jnp.bfloat16)
                    result += dot(both, cols_hot[r * tile_rows + i, pair], ((1,), (1,)))
                total[pl.ds(pl.multiple_of(h * CH, CH), CH), 2 * CH * pair : 2 * CH * (pair + 1)] = (
                    result[:CH] + result[CH:]
                )
            return carry

        lax.fori_loop(0, piece_tiles, tile_step, 0)
        decoded[here(m), :] = transform(total[...], tables, 1)
        result_copy(1, m).start()

    def here(m):
        return pl.ds(pl.multiple_of(m * chunk, chunk), chunk)

    def result_copy(kind, m):
        src, dst = ((mom, new_hbm), (decoded, dec_hbm))[kind]
        return pltpu.make_async_copy(src.at[here(m)], dst.at[here(m)], res_sem.at[kind, m])

    def own(m):
        q = z * pieces + m
        partial(q)

        @pl.when(z > 0)
        def _():
            add_arrived(q, 0, 1)

        @pl.when(z < lines - 1)
        def _():
            add_arrived(q, 1, -1)

        moment = 0.9 * mom[here(m), :] + acc[...].T
        coefficients = transform(moment, tables, 0)
        head, tail = split(coefficients)
        for h in range(piece_tiles):
            i = m * piece_tiles + h
            codes = lists[rep, i]
            picks = []
            for pair in range(pairs):
                at = (slice(h * CH, (h + 1) * CH), slice(2 * CH * pair, 2 * CH * (pair + 1)))
                cols = cols_hot[rep * tile_rows + i, pair]
                found = dot(jnp.concatenate([head[at], tail[at]], axis=0), cols)
                found = found[:CH] + found[CH:]
                row = row_codes(codes, pair)
                spots = lax.broadcasted_iota(jnp.int32, found.shape, 0)
                pick = jnp.sum(jnp.where(spots == row, found, 0.0), axis=0, keepdims=True)
                picks += [pick[:, : pick.shape[1] // 2], pick[:, pick.shape[1] // 2 :]]
            values[rep, i] = jnp.concatenate(picks, axis=0)
        for o in range(1, reps):
            value_copy(o, m).start()
        chosen = jnp.where(mask[here(m), :] > 0.5, coefficients, 0.0)
        mom[here(m), :] = moment - transform(chosen, tables, 1)
        result_copy(0, m).start()

    def late_step(m, carry):
        for k in (plain + 2 * m, plain + 2 * m + 1):
            line_step(k, 0)
        own(m)

        @pl.when(m > 0)
        def _():
            decode(m - 1)

        return carry

    lax.fori_loop(0, pieces, late_step, 0)
    decode(pieces - 1)

    for m in range(pieces):
        sib_copy(z * pieces + m).wait_send()
        for kind in range(2):
            result_copy(kind, m).wait()

    def left_step(k, carry):
        def wait(q):
            sib_copy(q).wait_send()

        each(k, wait, wait)
        return carry

    lax.fori_loop(0, steps, left_step, 0)
    for k in range(max(steps - 2, 0), steps):
        each(k, sent(0, 1), sent(1, -1))


def body(lines, reps, activations, out_grads, momentum, indices, counts):
    inputs, grads, moment, places = activations[0], out_grads[0], momentum[0], indices[0]
    tokens, model = inputs.shape
    owned, width = moment.shape
    tile_cols, slots = places.shape[1:]
    chunk = 4 * CH
    fill = -owned % chunk
    rows = owned + fill
    if fill:
        inputs = inputs.reshape(tokens, 2 * lines, owned)
        inputs = jnp.pad(inputs, ((0, 0), (0, 0), (0, fill))).reshape(tokens, 2 * lines * rows)
        moment = jnp.pad(moment, ((0, fill), (0, 0)))
        places = jnp.pad(places, ((0, fill // CH), (0, 0), (0, 0)), constant_values=-1)
    tile_rows = rows // CH
    pieces = rows // chunk
    count = lines * pieces
    sizes = (lines, reps, rows, chunk, pieces, width, tokens)
    vmem = pl.BlockSpec(memory_space=pltpu.VMEM)
    hbm = pl.BlockSpec(memory_space=pl.ANY)
    dma = pltpu.SemaphoreType.DMA
    new_moment, decoded = pl.pallas_call(
        functools.partial(kernel, sizes),
        out_shape=(
            jax.ShapeDtypeStruct((rows, width), jnp.float32),
            jax.ShapeDtypeStruct((rows, width), jnp.float32),
        ),
        in_specs=[vmem, hbm, hbm, hbm, vmem, vmem],
        out_specs=(hbm, hbm),
        scratch_shapes=[
            pltpu.VMEM((count, tokens, chunk), jnp.bfloat16),
            pltpu.VMEM((count, tokens, chunk), jnp.bfloat16),
            pltpu.VMEM((tokens, width), jnp.bfloat16),
            pltpu.VMEM((tokens, width), jnp.bfloat16),
            pltpu.VMEM((2, width, tokens), jnp.bfloat16),
            pltpu.VMEM((rows, width), jnp.float32),
            pltpu.VMEM((width, chunk), jnp.float32),
            pltpu.VMEM((count, width, chunk), jnp.int16),
            pltpu.VMEM((count, 1, chunk), jnp.float32),
            pltpu.VMEM((2, count, width, chunk), jnp.int16),
            pltpu.VMEM((2, count, 1, chunk), jnp.float32),
            pltpu.VMEM((reps, tile_rows, tile_cols, slots), jnp.int32),
            pltpu.VMEM((reps, tile_rows, tile_cols, slots), jnp.float32),
            pltpu.VMEM((rows, width), jnp.float32),
            pltpu.VMEM((reps * tile_rows, tile_cols // 2, 2 * CH, 2 * slots), jnp.bfloat16),
            pltpu.VMEM((chunk, width), jnp.float32),
            pltpu.VMEM((rows, width), jnp.float32),
            dma((count,)),
            dma((count,)),
            dma((count,)),
            dma((4,)),
            dma((2, count)),
            dma((2, 2, count)),
            dma((pieces + 1, reps)),
            dma((pieces + 1, reps)),
            dma((2, pieces)),
        ],
        compiler_params=pltpu.CompilerParams(
            collective_id=0, has_side_effects=True, vmem_limit_bytes=60 * 1024 * 1024
        ),
        cost_estimate=pl.CostEstimate(
            flops=2 * tokens * model * width, bytes_accessed=2 * tokens * model, transcendentals=0
        ),
    )(counts.reshape(1, 1), inputs, grads, moment, places, jnp.asarray(cosine_tables()))
    decoded = decoded[:owned]
    step_dir = decoded * lax.rsqrt(decoded * decoded + 0.04)
    return (new_moment[None, :owned], step_dir)


def solution(mesh):
    lines, reps = mesh.shape["fsdp"] // 2, mesh.shape["rep"]
    placed = (
        P("rep", "fsdp", None),
        P("rep", "fsdp", None),
        P("rep", "fsdp", None),
        P("rep", "fsdp", None, None),
        P("rep"),
    )
    return jax.shard_map(
        functools.partial(body, lines, reps),
        mesh=mesh,
        in_specs=placed,
        out_specs=(P("rep", "fsdp", None), P("fsdp", None)),
        check_vma=False,
    )
```

```python
import functools
import math

import jax
import jax.numpy as jnp
import numpy as np
from jax import lax
from jax.experimental import pallas as pl
from jax.experimental.pallas import tpu as pltpu
from jax.sharding import PartitionSpec as P
import ml_dtypes

CH = 64
MESH = pl.DeviceIdType.MESH
LEVELS = 32000.0


def cosine_tables():
    freq = np.arange(CH, dtype=np.float64)[:, None]
    place = np.arange(CH, dtype=np.float64)[None, :]
    table = np.cos(math.pi * (2 * place + 1) * freq / (2 * CH)) * math.sqrt(2.0 / CH)
    table[0] *= math.sqrt(0.5)
    whole = np.kron(np.eye(4), table).astype(np.float32)
    head = whole.astype(ml_dtypes.bfloat16)
    tail = (whole - head.astype(np.float32)).astype(ml_dtypes.bfloat16)
    return np.stack([head.T, tail.T, head, tail])


def split(value):
    head = value.astype(jnp.bfloat16)
    return head, (value - head.astype(jnp.float32)).astype(jnp.bfloat16)


def dot(a, b, contract=((1,), (0,))):
    return lax.dot_general(a, b, (contract, ((), ())), preferred_element_type=jnp.float32)


def transform(field, tables, way):
    height, width = field.shape
    rh, rl = tables[2 * way], tables[2 * way + 1]
    other = 2 - 2 * way
    lh, ll = tables[other, :height, :height], tables[other + 1, :height, :height]
    stack = jnp.concatenate([lh, ll], axis=0)
    parts = []
    for start in range(0, width, 256):
        fh, fl = split(field[:, start : start + 256])
        both = dot(jnp.concatenate([fh, fl], axis=0), rh)
        yh, yl = split(both[:height] + (dot(fh, rl) + both[height:]))
        both = dot(stack, yh)
        parts.append(both[:height] + (dot(lh, yl) + both[height:]))
    return jnp.concatenate(parts, axis=1)


def pair_rows(rows, pair):
    a = rows[2 * pair : 2 * pair + 1, :]
    b = rows[2 * pair + 1 : 2 * pair + 2, :]
    return a, b


def row_codes(rows, pair):
    a, b = pair_rows(rows, pair)
    return jnp.concatenate([a >> 6, b >> 6], axis=1)


def column_hot(rows, pair):
    a, b = pair_rows(rows, pair)
    codes = jnp.concatenate([a & 63, (b & 63) + 64], axis=1)
    spots = lax.broadcasted_iota(jnp.int32, (2 * CH, codes.shape[1]), 0)
    return jnp.where(spots == codes, 1.0, 0.0).astype(jnp.bfloat16)


def kernel(
    sizes,
    counts_ref, act_hbm, grad_hbm, mom_hbm, places_ref, tables,
    new_hbm, step_hbm,
    own_act, sib_act, own_grad, sib_grad, flipped, mom, acc, coded, scales, in_coded, in_scales,
    lists, values, mask, cols_hot, total, directions,
    act_sem, sib_send, sib_recv, misc_sem, out_send, out_recv, rep_send, rep_recv, res_sem,
):
    lines, reps, rows, chunk, pieces, width, tokens = sizes
    pairs = width // CH // 2
    tile_rows = rows // CH
    piece_tiles = chunk // CH
    f = lax.axis_index("fsdp")
    rep = lax.axis_index("rep")
    z, core = f // 2, f % 2
    sibling = {"fsdp": 2 * z + 1 - core}

    def along(step):
        return {"fsdp": 2 * (z + step) + core}

    grad_own = pltpu.make_async_copy(grad_hbm, own_grad, misc_sem.at[0])
    mom_own = pltpu.make_async_copy(mom_hbm, mom, misc_sem.at[1])
    grad_own.start()

    barrier = pltpu.get_barrier_semaphore()
    pl.semaphore_signal(barrier, inc=1, device_id=sibling, device_id_type=MESH)

    @pl.when(z > 0)
    def _():
        pl.semaphore_signal(barrier, inc=1, device_id=along(-1), device_id_type=MESH)

    @pl.when(z < lines - 1)
    def _():
        pl.semaphore_signal(barrier, inc=1, device_id=along(1), device_id_type=MESH)

    for o in range(1, reps):
        pl.semaphore_signal(
            barrier, inc=1, device_id={"rep": lax.rem(rep + o, reps)}, device_id_type=MESH
        )

    used = lax.broadcasted_iota(jnp.int32, places_ref.shape[1:], 1) < counts_ref[...]
    for i in range(tile_rows):
        lists[rep, i] = jnp.where(used, places_ref[i], -1)

    def source(q, lane):
        start = (2 * (q // pieces) + lane) * rows + (q % pieces) * chunk
        return act_hbm.at[:, pl.ds(pl.multiple_of(start, 128), chunk)]

    def own_copy(q):
        return pltpu.make_async_copy(source(q, core), own_act.at[q], act_sem.at[q])

    def sib_copy(q):
        return pltpu.make_async_remote_copy(
            src_ref=source(q, 1 - core), dst_ref=sib_act.at[q],
            send_sem=sib_send.at[q], recv_sem=sib_recv.at[q],
            device_id=sibling, device_id_type=MESH,
        )

    grad_sib = pltpu.make_async_remote_copy(
        src_ref=grad_hbm, dst_ref=sib_grad, send_sem=misc_sem.at[2], recv_sem=misc_sem.at[3],
        device_id=sibling, device_id_type=MESH,
    )

    steps = (lines - 1) * pieces
    plain = (lines - 3) * pieces

    def owner(k):
        later = k - plain
        block = jnp.where(later < 0, lines - 1 - k // pieces, 2 - later % 2)
        piece = jnp.where(later < 0, k % pieces, later // 2)
        return block, piece

    def each(tick, right, left):
        k = tick - z
        block, piece = owner(k)

        @pl.when((k >= 0) & (k < steps) & (block > z))
        def _():
            right(block * pieces + piece)

        j = tick - (lines - 1 - z)
        facing, part = owner(j)

        @pl.when((j >= 0) & (j < steps) & (lines - 1 - facing < z))
        def _():
            left((lines - 1 - facing) * pieces + part)

    def fetch(q):
        own_copy(q).start()
        sib_copy(q).start()

    neighbours = 1 + jnp.where(z > 0, 1, 0) + jnp.where(z < lines - 1, 1, 0) + (reps - 1)
    pl.semaphore_wait(barrier, neighbours)
    grad_sib.start()
    each(0, fetch, fetch)

    def list_copy(o):
        return pltpu.make_async_remote_copy(
            src_ref=lists.at[rep], dst_ref=lists.at[rep],
            send_sem=rep_send.at[pieces, o], recv_sem=rep_recv.at[pieces, o],
            device_id={"rep": lax.rem(rep + o, reps)}, device_id_type=MESH,
        )

    def value_copy(o, m):
        part = values.at[rep, pl.ds(m * piece_tiles, piece_tiles)]
        return pltpu.make_async_remote_copy(
            src_ref=part, dst_ref=part,
            send_sem=rep_send.at[m, o], recv_sem=rep_recv.at[m, o],
            device_id={"rep": lax.rem(rep + o, reps)}, device_id_type=MESH,
        )

    grad_own.wait()
    flipped[0] = own_grad[...].T
    grad_sib.wait()
    flipped[1] = sib_grad[...].T
    each(1, fetch, fetch)
    for o in range(1, reps):
        list_copy(o).start()

    def partial(q):
        own_copy(q).wait()
        sib_copy(q).wait_recv()
        acc[...] = dot(flipped[0], own_act[q]) + dot(flipped[1], sib_act[q])

    def chunk_copies(q, way, step):
        return [
            pltpu.make_async_remote_copy(
                src_ref=src.at[q], dst_ref=dst.at[way, q],
                send_sem=out_send.at[kind, q], recv_sem=out_recv.at[kind, way, q],
                device_id=along(step), device_id_type=MESH,
            )
            for kind, (src, dst) in enumerate(((coded, in_coded), (scales, in_scales)))
        ]

    def add_arrived(q, way, step):
        for copy in chunk_copies(q, way, step):
            copy.wait_recv()
        acc[...] += in_coded[way, q].astype(jnp.int32).astype(jnp.float32) * in_scales[way, q]

    def pass_on(q, way, step):
        value = acc[...]
        top = jnp.maximum(jnp.max(jnp.abs(value), axis=0, keepdims=True), 1e-30)
        scales[q] = top * (1.0 / LEVELS)
        coded[q] = jnp.round(value * (LEVELS / top)).astype(jnp.int32).astype(jnp.int16)
        for copy in chunk_copies(q, way, step):
            copy.start()

    def right(q):
        partial(q)

        @pl.when(z > 0)
        def _():
            add_arrived(q, 0, 1)

        pass_on(q, 0, 1)

    def left(q):
        partial(q)

        @pl.when(z < lines - 1)
        def _():
            add_arrived(q, 1, -1)

        pass_on(q, 1, -1)

    def sent(way, step):
        def wait(q):
            for copy in chunk_copies(q, way, step):
                copy.wait_send()

        return wait

    def line_step(k, carry):
        @pl.when(k >= 2)
        def _():
            each(k - 2, sent(0, 1), sent(1, -1))

        each(k + 2, fetch, fetch)

        @pl.when(k < pieces)
        def _():
            fetch(z * pieces + k)

        each(k, right, left)
        return carry

    def mask_step(i, carry):
        codes = lists[rep, i]
        for pair in range(pairs):
            row = row_codes(codes, pair)
            spots = lax.broadcasted_iota(jnp.int32, (CH, row.shape[1]), 0)
            hot = jnp.where(spots == row, 1.0, 0.0).astype(jnp.bfloat16)
            cols = column_hot(codes, pair)
            mask[pl.ds(pl.multiple_of(i * CH, CH), CH), 2 * CH * pair : 2 * CH * (pair + 1)] = (
                dot(hot, cols, ((1,), (1,)))
            )
        return carry

    def hot_step(n, carry):
        codes = lists[n // tile_rows, n % tile_rows]
        for pair in range(pairs):
            cols_hot[n, pair] = column_hot(codes, pair)
        return carry

    def prepare():
        mom_own.start()
        lax.fori_loop(0, tile_rows, mask_step, 0)
        for o in range(1, reps):
            list_copy(o).wait()
        lax.fori_loop(0, reps * tile_rows, hot_step, 0)
        mom_own.wait()

    middle = (z > 0) & (z < lines - 1)

    @pl.when(middle)
    def _():
        prepare()

    line_step(0, 0)

    @pl.when(jnp.logical_not(middle))
    def _():
        prepare()

    lax.fori_loop(1, plain + 1, line_step, 0)

    def decode(m):
        for o in range(1, reps):
            value_copy(o, m).wait()

        def tile_step(h, carry):
            i = m * piece_tiles + h
            for pair in range(pairs):
                result = jnp.zeros((2 * CH, 2 * CH), jnp.float32)
                for r in range(reps):
                    row = row_codes(lists[r, i], pair)
                    a, b = pair_rows(values[r, i], pair)
                    head, tail = split(jnp.concatenate([a, b], axis=1))
                    spots = lax.broadcasted_iota(jnp.int32, (CH, row.shape[1]), 0)
                    hit = spots == row
                    both = jnp.concatenate(
                        [
                            jnp.where(hit, head.astype(jnp.float32), 0.0),
                            jnp.where(hit, tail.astype(jnp.float32), 0.0),
                        ],
                        axis=0,
                    ).astype(jnp.bfloat16)
                    result += dot(both, cols_hot[r * tile_rows + i, pair], ((1,), (1,)))
                total[pl.ds(pl.multiple_of(h * CH, CH), CH), 2 * CH * pair : 2 * CH * (pair + 1)] = (
                    result[:CH] + result[CH:]
                )
            return carry

        lax.fori_loop(0, piece_tiles, tile_step, 0)
        result = transform(total[...], tables, 1)
        directions[here(m), :] = result * lax.rsqrt(result * result + 0.04)
        result_copy(1, m).start()

    def here(m):
        return pl.ds(pl.multiple_of(m * chunk, chunk), chunk)

    def result_copy(kind, m):
        src, dst = ((mom, new_hbm), (directions, step_hbm))[kind]
        return pltpu.make_async_copy(src.at[here(m)], dst.at[here(m)], res_sem.at[kind, m])

    def own(m):
        q = z * pieces + m
        partial(q)

        @pl.when(z > 0)
        def _():
            add_arrived(q, 0, 1)

        @pl.when(z < lines - 1)
        def _():
            add_arrived(q, 1, -1)

        moment = 0.9 * mom[here(m), :] + acc[...].T
        coefficients = transform(moment, tables, 0)
        head, tail = split(coefficients)
        for h in range(piece_tiles):
            i = m * piece_tiles + h
            codes = lists[rep, i]
            picks = []
            for pair in range(pairs):
                at = (slice(h * CH, (h + 1) * CH), slice(2 * CH * pair, 2 * CH * (pair + 1)))
                cols = cols_hot[rep * tile_rows + i, pair]
                found = dot(jnp.concatenate([head[at], tail[at]], axis=0), cols)
                found = found[:CH] + found[CH:]
                row = row_codes(codes, pair)
                spots = lax.broadcasted_iota(jnp.int32, found.shape, 0)
                pick = jnp.sum(jnp.where(spots == row, found, 0.0), axis=0, keepdims=True)
                picks += [pick[:, : pick.shape[1] // 2], pick[:, pick.shape[1] // 2 :]]
            values[rep, i] = jnp.concatenate(picks, axis=0)
        for o in range(1, reps):
            value_copy(o, m).start()
        chosen = jnp.where(mask[here(m), :] > 0.5, coefficients, 0.0)
        mom[here(m), :] = moment - transform(chosen, tables, 1)
        result_copy(0, m).start()

    def late_step(m, carry):
        for k in (plain + 2 * m + 1, plain + 2 * m + 2):
            line_step(k, 0)
        own(m)

        @pl.when(m > 0)
        def _():
            decode(m - 1)

        return carry

    lax.fori_loop(0, pieces, late_step, 0)
    decode(pieces - 1)

    for m in range(pieces):
        sib_copy(z * pieces + m).wait_send()
        for kind in range(2):
            result_copy(kind, m).wait()

    def left_step(k, carry):
        def wait(q):
            sib_copy(q).wait_send()

        each(k, wait, wait)
        return carry

    lax.fori_loop(0, steps + 1, left_step, 0)
    for k in (steps - 1, steps):
        each(k, sent(0, 1), sent(1, -1))


def body(lines, reps, activations, out_grads, momentum, indices, counts):
    inputs, grads, moment, places = activations[0], out_grads[0], momentum[0], indices[0]
    tokens, model = inputs.shape
    owned, width = moment.shape
    tile_cols, slots = places.shape[1:]
    chunk = 4 * CH
    fill = -owned % chunk
    rows = owned + fill
    if fill:
        inputs = inputs.reshape(tokens, 2 * lines, owned)
        inputs = jnp.pad(inputs, ((0, 0), (0, 0), (0, fill))).reshape(tokens, 2 * lines * rows)
        moment = jnp.pad(moment, ((0, fill), (0, 0)))
        places = jnp.pad(places, ((0, fill // CH), (0, 0), (0, 0)), constant_values=-1)
    tile_rows = rows // CH
    pieces = rows // chunk
    count = lines * pieces
    sizes = (lines, reps, rows, chunk, pieces, width, tokens)
    vmem = pl.BlockSpec(memory_space=pltpu.VMEM)
    hbm = pl.BlockSpec(memory_space=pl.ANY)
    dma = pltpu.SemaphoreType.DMA
    new_moment, step_dir = pl.pallas_call(
        functools.partial(kernel, sizes),
        out_shape=(
            jax.ShapeDtypeStruct((rows, width), jnp.float32),
            jax.ShapeDtypeStruct((rows, width), jnp.float32),
        ),
        in_specs=[vmem, hbm, hbm, hbm, vmem, vmem],
        out_specs=(hbm, hbm),
        scratch_shapes=[
            pltpu.VMEM((count, tokens, chunk), jnp.bfloat16),
            pltpu.VMEM((count, tokens, chunk), jnp.bfloat16),
            pltpu.VMEM((tokens, width), jnp.bfloat16),
            pltpu.VMEM((tokens, width), jnp.bfloat16),
            pltpu.VMEM((2, width, tokens), jnp.bfloat16),
            pltpu.VMEM((rows, width), jnp.float32),
            pltpu.VMEM((width, chunk), jnp.float32),
            pltpu.VMEM((count, width, chunk), jnp.int16),
            pltpu.VMEM((count, 1, chunk), jnp.float32),
            pltpu.VMEM((2, count, width, chunk), jnp.int16),
            pltpu.VMEM((2, count, 1, chunk), jnp.float32),
            pltpu.VMEM((reps, tile_rows, tile_cols, slots), jnp.int32),
            pltpu.VMEM((reps, tile_rows, tile_cols, slots), jnp.float32),
            pltpu.VMEM((rows, width), jnp.float32),
            pltpu.VMEM((reps * tile_rows, tile_cols // 2, 2 * CH, 2 * slots), jnp.bfloat16),
            pltpu.VMEM((chunk, width), jnp.float32),
            pltpu.VMEM((rows, width), jnp.float32),
            dma((count,)),
            dma((count,)),
            dma((count,)),
            dma((4,)),
            dma((2, count)),
            dma((2, 2, count)),
            dma((pieces + 1, reps)),
            dma((pieces + 1, reps)),
            dma((2, pieces)),
        ],
        compiler_params=pltpu.CompilerParams(
            collective_id=0, has_side_effects=True, vmem_limit_bytes=60 * 1024 * 1024
        ),
        cost_estimate=pl.CostEstimate(
            flops=2 * tokens * model * width, bytes_accessed=2 * tokens * model, transcendentals=0
        ),
    )(counts.reshape(1, 1), inputs, grads, moment, places, jnp.asarray(cosine_tables()))
    return (new_moment[None, :owned], step_dir[:owned])


def solution(mesh):
    lines, reps = mesh.shape["fsdp"] // 2, mesh.shape["rep"]
    placed = (
        P("rep", "fsdp", None),
        P("rep", "fsdp", None),
        P("rep", "fsdp", None),
        P("rep", "fsdp", None, None),
        P("rep"),
    )
    return jax.shard_map(
        functools.partial(body, lines, reps),
        mesh=mesh,
        in_specs=placed,
        out_specs=(P("rep", "fsdp", None), P("fsdp", None)),
        check_vma=False,
    )
```

```python
import functools
import math

import jax
import jax.numpy as jnp
import numpy as np
from jax import lax
from jax.experimental import pallas as pl
from jax.experimental.pallas import tpu as pltpu
from jax.sharding import PartitionSpec as P
import ml_dtypes

CH = 64
MESH = pl.DeviceIdType.MESH
LEVELS = 32000.0


def cosine_tables():
    freq = np.arange(CH, dtype=np.float64)[:, None]
    place = np.arange(CH, dtype=np.float64)[None, :]
    table = np.cos(math.pi * (2 * place + 1) * freq / (2 * CH)) * math.sqrt(2.0 / CH)
    table[0] *= math.sqrt(0.5)
    whole = np.kron(np.eye(4), table).astype(np.float32)
    head = whole.astype(ml_dtypes.bfloat16)
    tail = (whole - head.astype(np.float32)).astype(ml_dtypes.bfloat16)
    return np.stack([head.T, tail.T, head, tail])


def split(value):
    head = value.astype(jnp.bfloat16)
    return head, (value - head.astype(jnp.float32)).astype(jnp.bfloat16)


def dot(a, b, contract=((1,), (0,))):
    return lax.dot_general(a, b, (contract, ((), ())), preferred_element_type=jnp.float32)


def transform(field, tables, way):
    height, width = field.shape
    rh, rl = tables[2 * way], tables[2 * way + 1]
    other = 2 - 2 * way
    lh, ll = tables[other, :height, :height], tables[other + 1, :height, :height]
    stack = jnp.concatenate([lh, ll], axis=0)
    parts = []
    for start in range(0, width, 256):
        fh, fl = split(field[:, start : start + 256])
        both = dot(jnp.concatenate([fh, fl], axis=0), rh)
        yh, yl = split(both[:height] + (dot(fh, rl) + both[height:]))
        both = dot(stack, yh)
        parts.append(both[:height] + (dot(lh, yl) + both[height:]))
    return jnp.concatenate(parts, axis=1)


def pair_rows(rows, pair):
    a = rows[2 * pair : 2 * pair + 1, :]
    b = rows[2 * pair + 1 : 2 * pair + 2, :]
    return a, b


def row_codes(rows, pair):
    a, b = pair_rows(rows, pair)
    return jnp.concatenate([a >> 6, b >> 6], axis=1)


def column_hot(rows, pair):
    a, b = pair_rows(rows, pair)
    codes = jnp.concatenate([a & 63, (b & 63) + 64], axis=1)
    spots = lax.broadcasted_iota(jnp.int32, (2 * CH, codes.shape[1]), 0)
    return jnp.where(spots == codes, 1.0, 0.0).astype(jnp.bfloat16)


def kernel(
    sizes,
    counts_ref, act_hbm, grad_hbm, mom_hbm, places_ref, tables,
    mom, directions,
    own_act, sib_act, own_grad, sib_grad, flipped, acc, coded, scales, in_coded, in_scales,
    lists, values, mask, cols_hot, total,
    act_sem, sib_send, sib_recv, misc_sem, out_send, out_recv, rep_send, rep_recv,
):
    lines, reps, rows, chunk, pieces, width, tokens = sizes
    pairs = width // CH // 2
    tile_rows = rows // CH
    piece_tiles = chunk // CH
    f = lax.axis_index("fsdp")
    rep = lax.axis_index("rep")
    z, core = f // 2, f % 2
    sibling = {"fsdp": 2 * z + 1 - core}

    def along(step):
        return {"fsdp": 2 * (z + step) + core}

    grad_own = pltpu.make_async_copy(grad_hbm, own_grad, misc_sem.at[0])
    mom_own = pltpu.make_async_copy(mom_hbm, mom, misc_sem.at[1])
    grad_own.start()

    barrier = pltpu.get_barrier_semaphore()
    pl.semaphore_signal(barrier, inc=1, device_id=sibling, device_id_type=MESH)

    @pl.when(z > 0)
    def _():
        pl.semaphore_signal(barrier, inc=1, device_id=along(-1), device_id_type=MESH)

    @pl.when(z < lines - 1)
    def _():
        pl.semaphore_signal(barrier, inc=1, device_id=along(1), device_id_type=MESH)

    for o in range(1, reps):
        pl.semaphore_signal(
            barrier, inc=1, device_id={"rep": lax.rem(rep + o, reps)}, device_id_type=MESH
        )

    used = lax.broadcasted_iota(jnp.int32, places_ref.shape[1:], 1) < counts_ref[...]
    for i in range(tile_rows):
        lists[rep, i] = jnp.where(used, places_ref[i], -1)

    def source(q, lane):
        start = (2 * (q // pieces) + lane) * rows + (q % pieces) * chunk
        return act_hbm.at[:, pl.ds(pl.multiple_of(start, 128), chunk)]

    def own_copy(q):
        return pltpu.make_async_copy(source(q, core), own_act.at[q], act_sem.at[q])

    def sib_copy(q):
        return pltpu.make_async_remote_copy(
            src_ref=source(q, 1 - core), dst_ref=sib_act.at[q],
            send_sem=sib_send.at[q], recv_sem=sib_recv.at[q],
            device_id=sibling, device_id_type=MESH,
        )

    grad_sib = pltpu.make_async_remote_copy(
        src_ref=grad_hbm, dst_ref=sib_grad, send_sem=misc_sem.at[2], recv_sem=misc_sem.at[3],
        device_id=sibling, device_id_type=MESH,
    )

    steps = (lines - 1) * pieces
    plain = (lines - 3) * pieces

    def owner(k):
        later = k - plain
        block = jnp.where(later < 0, lines - 1 - k // pieces, 2 - later % 2)
        piece = jnp.where(later < 0, k % pieces, later // 2)
        return block, piece

    def each(tick, right, left):
        k = tick - z
        block, piece = owner(k)

        @pl.when((k >= 0) & (k < steps) & (block > z))
        def _():
            right(block * pieces + piece)

        j = tick - (lines - 1 - z)
        facing, part = owner(j)

        @pl.when((j >= 0) & (j < steps) & (lines - 1 - facing < z))
        def _():
            left((lines - 1 - facing) * pieces + part)

    def fetch(q):
        own_copy(q).start()
        sib_copy(q).start()

    neighbours = 1 + jnp.where(z > 0, 1, 0) + jnp.where(z < lines - 1, 1, 0) + (reps - 1)
    pl.semaphore_wait(barrier, neighbours)
    grad_sib.start()
    each(0, fetch, fetch)

    def list_copy(o):
        return pltpu.make_async_remote_copy(
            src_ref=lists.at[rep], dst_ref=lists.at[rep],
            send_sem=rep_send.at[pieces, o], recv_sem=rep_recv.at[pieces, o],
            device_id={"rep": lax.rem(rep + o, reps)}, device_id_type=MESH,
        )

    def value_copy(o, m):
        part = values.at[rep, pl.ds(m * piece_tiles, piece_tiles)]
        return pltpu.make_async_remote_copy(
            src_ref=part, dst_ref=part,
            send_sem=rep_send.at[m, o], recv_sem=rep_recv.at[m, o],
            device_id={"rep": lax.rem(rep + o, reps)}, device_id_type=MESH,
        )

    grad_own.wait()
    flipped[0] = own_grad[...].T
    grad_sib.wait()
    flipped[1] = sib_grad[...].T
    each(1, fetch, fetch)
    for o in range(1, reps):
        list_copy(o).start()

    def partial(q):
        own_copy(q).wait()
        sib_copy(q).wait_recv()
        acc[...] = dot(flipped[0], own_act[q]) + dot(flipped[1], sib_act[q])

    def chunk_copies(q, way, step):
        return [
            pltpu.make_async_remote_copy(
                src_ref=src.at[q], dst_ref=dst.at[way, q],
                send_sem=out_send.at[kind, q], recv_sem=out_recv.at[kind, way, q],
                device_id=along(step), device_id_type=MESH,
            )
            for kind, (src, dst) in enumerate(((coded, in_coded), (scales, in_scales)))
        ]

    def add_arrived(q, way, step):
        for copy in chunk_copies(q, way, step):
            copy.wait_recv()
        acc[...] += in_coded[way, q].astype(jnp.int32).astype(jnp.float32) * in_scales[way, q]

    def pass_on(q, way, step):
        value = acc[...]
        top = jnp.maximum(jnp.max(jnp.abs(value), axis=0, keepdims=True), 1e-30)
        scales[q] = top * (1.0 / LEVELS)
        coded[q] = jnp.round(value * (LEVELS / top)).astype(jnp.int32).astype(jnp.int16)
        for copy in chunk_copies(q, way, step):
            copy.start()

    def right(q):
        partial(q)

        @pl.when(z > 0)
        def _():
            add_arrived(q, 0, 1)

        pass_on(q, 0, 1)

    def left(q):
        partial(q)

        @pl.when(z < lines - 1)
        def _():
            add_arrived(q, 1, -1)

        pass_on(q, 1, -1)

    def sent(way, step):
        def wait(q):
            for copy in chunk_copies(q, way, step):
                copy.wait_send()

        return wait

    def line_step(k, carry):
        @pl.when(k >= 2)
        def _():
            each(k - 2, sent(0, 1), sent(1, -1))

        each(k + 2, fetch, fetch)

        @pl.when(k < pieces)
        def _():
            fetch(z * pieces + k)

        each(k, right, left)
        return carry

    def mask_step(i, carry):
        codes = lists[rep, i]
        for pair in range(pairs):
            row = row_codes(codes, pair)
            spots = lax.broadcasted_iota(jnp.int32, (CH, row.shape[1]), 0)
            hot = jnp.where(spots == row, 1.0, 0.0).astype(jnp.bfloat16)
            cols = column_hot(codes, pair)
            mask[pl.ds(pl.multiple_of(i * CH, CH), CH), 2 * CH * pair : 2 * CH * (pair + 1)] = (
                dot(hot, cols, ((1,), (1,)))
            )
        return carry

    def hot_step(n, carry):
        codes = lists[n // tile_rows, n % tile_rows]
        for pair in range(pairs):
            cols_hot[n, pair] = column_hot(codes, pair)
        return carry

    def prepare():
        mom_own.start()
        lax.fori_loop(0, tile_rows, mask_step, 0)
        for o in range(1, reps):
            list_copy(o).wait()
        lax.fori_loop(0, reps * tile_rows, hot_step, 0)
        mom_own.wait()

    middle = (z > 0) & (z < lines - 1)

    @pl.when(middle)
    def _():
        prepare()

    line_step(0, 0)

    @pl.when(jnp.logical_not(middle))
    def _():
        prepare()

    lax.fori_loop(1, plain + 1, line_step, 0)

    def decode(m):
        for o in range(1, reps):
            value_copy(o, m).wait()

        def tile_step(h, carry):
            i = m * piece_tiles + h
            for pair in range(pairs):
                result = jnp.zeros((2 * CH, 2 * CH), jnp.float32)
                for r in range(reps):
                    row = row_codes(lists[r, i], pair)
                    a, b = pair_rows(values[r, i], pair)
                    head, tail = split(jnp.concatenate([a, b], axis=1))
                    spots = lax.broadcasted_iota(jnp.int32, (CH, row.shape[1]), 0)
                    hit = spots == row
                    both = jnp.concatenate(
                        [
                            jnp.where(hit, head.astype(jnp.float32), 0.0),
                            jnp.where(hit, tail.astype(jnp.float32), 0.0),
                        ],
                        axis=0,
                    ).astype(jnp.bfloat16)
                    result += dot(both, cols_hot[r * tile_rows + i, pair], ((1,), (1,)))
                total[pl.ds(pl.multiple_of(h * CH, CH), CH), 2 * CH * pair : 2 * CH * (pair + 1)] = (
                    result[:CH] + result[CH:]
                )
            return carry

        lax.fori_loop(0, piece_tiles, tile_step, 0)
        result = transform(total[...], tables, 1)
        directions[here(m), :] = result * lax.rsqrt(result * result + 0.04)

    def here(m):
        return pl.ds(pl.multiple_of(m * chunk, chunk), chunk)

    def own(m):
        q = z * pieces + m
        partial(q)

        @pl.when(z > 0)
        def _():
            add_arrived(q, 0, 1)

        @pl.when(z < lines - 1)
        def _():
            add_arrived(q, 1, -1)

        moment = 0.9 * mom[here(m), :] + acc[...].T
        coefficients = transform(moment, tables, 0)
        head, tail = split(coefficients)
        for h in range(piece_tiles):
            i = m * piece_tiles + h
            codes = lists[rep, i]
            picks = []
            for pair in range(pairs):
                at = (slice(h * CH, (h + 1) * CH), slice(2 * CH * pair, 2 * CH * (pair + 1)))
                cols = cols_hot[rep * tile_rows + i, pair]
                found = dot(jnp.concatenate([head[at], tail[at]], axis=0), cols)
                found = found[:CH] + found[CH:]
                row = row_codes(codes, pair)
                spots = lax.broadcasted_iota(jnp.int32, found.shape, 0)
                pick = jnp.sum(jnp.where(spots == row, found, 0.0), axis=0, keepdims=True)
                picks += [pick[:, : pick.shape[1] // 2], pick[:, pick.shape[1] // 2 :]]
            values[rep, i] = jnp.concatenate(picks, axis=0)
        for o in range(1, reps):
            value_copy(o, m).start()
        chosen = jnp.where(mask[here(m), :] > 0.5, coefficients, 0.0)
        mom[here(m), :] = moment - transform(chosen, tables, 1)

    def late_step(m, carry):
        for k in (plain + 2 * m + 1, plain + 2 * m + 2):
            line_step(k, 0)

        @pl.when(m > 0)
        def _():
            decode(m - 1)

        own(m)
        return carry

    lax.fori_loop(0, pieces, late_step, 0)
    decode(pieces - 1)

    for m in range(pieces):
        sib_copy(z * pieces + m).wait_send()

    def left_step(k, carry):
        def wait(q):
            sib_copy(q).wait_send()

        each(k, wait, wait)
        return carry

    lax.fori_loop(0, steps + 1, left_step, 0)
    for k in (steps - 1, steps):
        each(k, sent(0, 1), sent(1, -1))


def body(lines, reps, activations, out_grads, momentum, indices, counts):
    inputs, grads, moment, places = activations[0], out_grads[0], momentum[0], indices[0]
    tokens, model = inputs.shape
    owned, width = moment.shape
    tile_cols, slots = places.shape[1:]
    chunk = 4 * CH
    fill = -owned % chunk
    rows = owned + fill
    if fill:
        inputs = inputs.reshape(tokens, 2 * lines, owned)
        inputs = jnp.pad(inputs, ((0, 0), (0, 0), (0, fill))).reshape(tokens, 2 * lines * rows)
        moment = jnp.pad(moment, ((0, fill), (0, 0)))
        places = jnp.pad(places, ((0, fill // CH), (0, 0), (0, 0)), constant_values=-1)
    tile_rows = rows // CH
    pieces = rows // chunk
    count = lines * pieces
    sizes = (lines, reps, rows, chunk, pieces, width, tokens)
    vmem = pl.BlockSpec(memory_space=pltpu.VMEM)
    hbm = pl.BlockSpec(memory_space=pltpu.HBM)
    dma = pltpu.SemaphoreType.DMA
    new_moment, step_dir = pl.pallas_call(
        functools.partial(kernel, sizes),
        out_shape=(
            pltpu.VMEM((rows, width), jnp.float32),
            pltpu.VMEM((rows, width), jnp.float32),
        ),
        in_specs=[vmem, hbm, hbm, hbm, vmem, vmem],
        out_specs=(vmem, vmem),
        scratch_shapes=[
            pltpu.VMEM((count, tokens, chunk), jnp.bfloat16),
            pltpu.VMEM((count, tokens, chunk), jnp.bfloat16),
            pltpu.VMEM((tokens, width), jnp.bfloat16),
            pltpu.VMEM((tokens, width), jnp.bfloat16),
            pltpu.VMEM((2, width, tokens), jnp.bfloat16),
            pltpu.VMEM((width, chunk), jnp.float32),
            pltpu.VMEM((count, width, chunk), jnp.int16),
            pltpu.VMEM((count, 1, chunk), jnp.float32),
            pltpu.VMEM((2, count, width, chunk), jnp.int16),
            pltpu.VMEM((2, count, 1, chunk), jnp.float32),
            pltpu.VMEM((reps, tile_rows, tile_cols, slots), jnp.int32),
            pltpu.VMEM((reps, tile_rows, tile_cols, slots), jnp.float32),
            pltpu.VMEM((rows, width), jnp.float32),
            pltpu.VMEM((reps * tile_rows, tile_cols // 2, 2 * CH, 2 * slots), jnp.bfloat16),
            pltpu.VMEM((chunk, width), jnp.float32),
            dma((count,)),
            dma((count,)),
            dma((count,)),
            dma((4,)),
            dma((2, count)),
            dma((2, 2, count)),
            dma((pieces + 1, reps)),
            dma((pieces + 1, reps)),
        ],
        compiler_params=pltpu.CompilerParams(
            collective_id=0, has_side_effects=True, vmem_limit_bytes=48 * 1024 * 1024
        ),
        cost_estimate=pl.CostEstimate(
            flops=2 * tokens * model * width, bytes_accessed=2 * tokens * model, transcendentals=0
        ),
    )(counts.reshape(1, 1), inputs, grads, moment, places, jnp.asarray(cosine_tables()))
    return (new_moment[None, :owned], step_dir[:owned])


def solution(mesh):
    lines, reps = mesh.shape["fsdp"] // 2, mesh.shape["rep"]
    placed = (
        P("rep", "fsdp", None),
        P("rep", "fsdp", None),
        P("rep", "fsdp", None),
        P("rep", "fsdp", None, None),
        P("rep"),
    )
    return jax.shard_map(
        functools.partial(body, lines, reps),
        mesh=mesh,
        in_specs=placed,
        out_specs=(P("rep", "fsdp", None), P("fsdp", None)),
        check_vma=False,
    )
```

```python
import functools
import math

import jax
import jax.numpy as jnp
import numpy as np
from jax import lax
from jax.experimental import pallas as pl
from jax.experimental.pallas import tpu as pltpu
from jax.sharding import PartitionSpec as P
import ml_dtypes

CH = 64
MESH = pl.DeviceIdType.MESH
LEVELS = 32000.0
DEPTH = 3


def cosine_tables():
    freq = np.arange(CH, dtype=np.float64)[:, None]
    place = np.arange(CH, dtype=np.float64)[None, :]
    table = np.cos(math.pi * (2 * place + 1) * freq / (2 * CH)) * math.sqrt(2.0 / CH)
    table[0] *= math.sqrt(0.5)
    whole = np.kron(np.eye(4), table).astype(np.float32)
    head = whole.astype(ml_dtypes.bfloat16)
    tail = (whole - head.astype(np.float32)).astype(ml_dtypes.bfloat16)
    return np.stack([head.T, tail.T, head, tail])


def split(value):
    head = value.astype(jnp.bfloat16)
    return head, (value - head.astype(jnp.float32)).astype(jnp.bfloat16)


def dot(a, b, contract=((1,), (0,))):
    return lax.dot_general(a, b, (contract, ((), ())), preferred_element_type=jnp.float32)


def transform(field, tables, way):
    height, width = field.shape
    rh, rl = tables[2 * way], tables[2 * way + 1]
    other = 2 - 2 * way
    lh, ll = tables[other, :height, :height], tables[other + 1, :height, :height]
    stack = jnp.concatenate([lh, ll], axis=0)
    parts = []
    for start in range(0, width, 256):
        fh, fl = split(field[:, start : start + 256])
        both = dot(jnp.concatenate([fh, fl], axis=0), rh)
        yh, yl = split(both[:height] + (dot(fh, rl) + both[height:]))
        both = dot(stack, yh)
        parts.append(both[:height] + (dot(lh, yl) + both[height:]))
    return jnp.concatenate(parts, axis=1)


def pair_rows(rows, pair):
    a = rows[2 * pair : 2 * pair + 1, :]
    b = rows[2 * pair + 1 : 2 * pair + 2, :]
    return a, b


def row_codes(rows, pair):
    a, b = pair_rows(rows, pair)
    return jnp.concatenate([a >> 6, b >> 6], axis=1)


def column_hot(rows, pair):
    a, b = pair_rows(rows, pair)
    codes = jnp.concatenate([a & 63, (b & 63) + 64], axis=1)
    spots = lax.broadcasted_iota(jnp.int32, (2 * CH, codes.shape[1]), 0)
    return jnp.where(spots == codes, 1.0, 0.0).astype(jnp.bfloat16)


def kernel(
    sizes,
    counts_ref, act_hbm, grad_hbm, mom_hbm, places_ref, tables_hbm,
    mom, directions,
    own_act, sib_act, own_grad, sib_grad, flipped, acc, coded, scales, in_coded, in_scales,
    lists, values, mask, cols_hot, total, tables,
    act_sem, sib_send, sib_recv, misc_sem, out_send, out_recv, rep_send, rep_recv,
):
    lines, reps, rows, chunk, pieces, width, tokens = sizes
    pairs = width // CH // 2
    tile_rows = rows // CH
    piece_tiles = chunk // CH
    span = 2 * lists.shape[-1]
    f = lax.axis_index("fsdp")
    rep = lax.axis_index("rep")
    z, core = f // 2, f % 2
    sibling = {"fsdp": 2 * z + 1 - core}

    def along(step):
        return {"fsdp": 2 * (z + step) + core}

    grad_own = pltpu.make_async_copy(grad_hbm, own_grad, misc_sem.at[0])
    mom_own = pltpu.make_async_copy(mom_hbm, mom, misc_sem.at[1])
    tables_own = pltpu.make_async_copy(tables_hbm, tables, misc_sem.at[4])
    grad_own.start()

    barrier = pltpu.get_barrier_semaphore()
    pl.semaphore_signal(barrier, inc=1, device_id=sibling, device_id_type=MESH)

    @pl.when(z > 0)
    def _():
        pl.semaphore_signal(barrier, inc=1, device_id=along(-1), device_id_type=MESH)

    @pl.when(z < lines - 1)
    def _():
        pl.semaphore_signal(barrier, inc=1, device_id=along(1), device_id_type=MESH)

    for o in range(1, reps):
        pl.semaphore_signal(
            barrier, inc=1, device_id={"rep": lax.rem(rep + o, reps)}, device_id_type=MESH
        )

    used = lax.broadcasted_iota(jnp.int32, places_ref.shape[1:], 1) < counts_ref[...]
    for i in range(tile_rows):
        lists[rep, i] = jnp.where(used, places_ref[i], -1)

    def source(q, lane):
        start = (2 * (q // pieces) + lane) * rows + (q % pieces) * chunk
        return act_hbm.at[:, pl.ds(pl.multiple_of(start, 128), chunk)]

    def own_copy(q):
        return pltpu.make_async_copy(source(q, core), own_act.at[q], act_sem.at[q])

    def sib_copy(q):
        return pltpu.make_async_remote_copy(
            src_ref=source(q, 1 - core), dst_ref=sib_act.at[q],
            send_sem=sib_send.at[q], recv_sem=sib_recv.at[q],
            device_id=sibling, device_id_type=MESH,
        )

    grad_sib = pltpu.make_async_remote_copy(
        src_ref=grad_hbm, dst_ref=sib_grad, send_sem=misc_sem.at[2], recv_sem=misc_sem.at[3],
        device_id=sibling, device_id_type=MESH,
    )

    steps = (lines - 1) * pieces
    plain = (lines - 3) * pieces

    def owner(k):
        later = k - plain
        block = jnp.where(later < 0, lines - 1 - k // pieces, 2 - later % 2)
        piece = jnp.where(later < 0, k % pieces, later // 2)
        return block, piece

    def each(tick, right, left):
        k = tick - z
        block, piece = owner(k)

        @pl.when((k >= 0) & (k < steps) & (block > z))
        def _():
            right(block * pieces + piece)

        j = tick - (lines - 1 - z)
        facing, part = owner(j)

        @pl.when((j >= 0) & (j < steps) & (lines - 1 - facing < z))
        def _():
            left((lines - 1 - facing) * pieces + part)

    def fetch(q):
        own_copy(q).start()
        sib_copy(q).start()

    neighbours = 1 + jnp.where(z > 0, 1, 0) + jnp.where(z < lines - 1, 1, 0) + (reps - 1)
    pl.semaphore_wait(barrier, neighbours)
    grad_sib.start()
    each(0, fetch, fetch)

    def list_copy(o):
        return pltpu.make_async_remote_copy(
            src_ref=lists.at[rep], dst_ref=lists.at[rep],
            send_sem=rep_send.at[pieces, o], recv_sem=rep_recv.at[pieces, o],
            device_id={"rep": lax.rem(rep + o, reps)}, device_id_type=MESH,
        )

    def value_copy(o, m):
        part = values.at[rep, pl.ds(m * piece_tiles, piece_tiles)]
        return pltpu.make_async_remote_copy(
            src_ref=part, dst_ref=part,
            send_sem=rep_send.at[m, o], recv_sem=rep_recv.at[m, o],
            device_id={"rep": lax.rem(rep + o, reps)}, device_id_type=MESH,
        )

    grad_own.wait()
    flipped[0] = own_grad[...].T
    grad_sib.wait()
    flipped[1] = sib_grad[...].T
    each(1, fetch, fetch)
    for o in range(1, reps):
        list_copy(o).start()

    def partial(q):
        own_copy(q).wait()
        sib_copy(q).wait_recv()
        acc[...] = dot(flipped[0], own_act[q]) + dot(flipped[1], sib_act[q])

    def chunk_copies(q, way, step):
        return [
            pltpu.make_async_remote_copy(
                src_ref=src.at[q], dst_ref=dst.at[way, q],
                send_sem=out_send.at[kind, q], recv_sem=out_recv.at[kind, way, q],
                device_id=along(step), device_id_type=MESH,
            )
            for kind, (src, dst) in enumerate(((coded, in_coded), (scales, in_scales)))
        ]

    def add_arrived(q, way, step):
        for copy in chunk_copies(q, way, step):
            copy.wait_recv()
        acc[...] += in_coded[way, q].astype(jnp.int32).astype(jnp.float32) * in_scales[way, q]

    def pass_on(q, way, step):
        value = acc[...]
        top = jnp.maximum(jnp.max(jnp.abs(value), axis=0, keepdims=True), 1e-30)
        scales[q] = top * (1.0 / LEVELS)
        coded[q] = jnp.round(value * (LEVELS / top)).astype(jnp.int32).astype(jnp.int16)
        for copy in chunk_copies(q, way, step):
            copy.start()

    def right(q):
        partial(q)

        @pl.when(z > 0)
        def _():
            add_arrived(q, 0, 1)

        pass_on(q, 0, 1)

    def left(q):
        partial(q)

        @pl.when(z < lines - 1)
        def _():
            add_arrived(q, 1, -1)

        pass_on(q, 1, -1)

    def sent(way, step):
        def wait(q):
            for copy in chunk_copies(q, way, step):
                copy.wait_send()

        return wait

    def line_step(k, carry):
        each(k - DEPTH, sent(0, 1), sent(1, -1))

        each(k + 2, fetch, fetch)

        @pl.when(k < pieces)
        def _():
            fetch(z * pieces + k)

        each(k, right, left)
        return carry

    def mask_step(i, carry):
        codes = lists[rep, i]
        for pair in range(pairs):
            row = row_codes(codes, pair)
            spots = lax.broadcasted_iota(jnp.int32, (CH, row.shape[1]), 0)
            hot = jnp.where(spots == row, 1.0, 0.0).astype(jnp.bfloat16)
            cols = column_hot(codes, pair)
            mask[pl.ds(pl.multiple_of(i * CH, CH), CH), 2 * CH * pair : 2 * CH * (pair + 1)] = (
                dot(hot, cols, ((1,), (1,)))
            )
        return carry

    def hot_step(n, carry):
        for r in range(reps):
            for pair in range(pairs):
                cols_hot[n, pair, :, r * span : (r + 1) * span] = column_hot(lists[r, n], pair)
        return carry

    def prepare():
        mom_own.start()
        tables_own.start()
        lax.fori_loop(0, tile_rows, mask_step, 0)
        for o in range(1, reps):
            list_copy(o).wait()
        lax.fori_loop(0, tile_rows, hot_step, 0)
        mom_own.wait()
        tables_own.wait()

    middle = (z > 0) & (z < lines - 1)

    @pl.when(middle)
    def _():
        prepare()

    line_step(0, 0)

    @pl.when(jnp.logical_not(middle))
    def _():
        prepare()

    lax.fori_loop(1, plain + 1, line_step, 0)

    def decode(m):
        for o in range(1, reps):
            value_copy(o, m).wait()

        def tile_step(h, carry):
            i = m * piece_tiles + h
            for pair in range(pairs):
                parts = []
                for r in range(reps):
                    row = row_codes(lists[r, i], pair)
                    a, b = pair_rows(values[r, i], pair)
                    head, tail = split(jnp.concatenate([a, b], axis=1))
                    spots = lax.broadcasted_iota(jnp.int32, (CH, row.shape[1]), 0)
                    hit = spots == row
                    both = jnp.concatenate(
                        [
                            jnp.where(hit, head.astype(jnp.float32), 0.0),
                            jnp.where(hit, tail.astype(jnp.float32), 0.0),
                        ],
                        axis=0,
                    ).astype(jnp.bfloat16)
                    parts.append(both)
                result = dot(jnp.concatenate(parts, axis=1), cols_hot[i, pair], ((1,), (1,)))
                total[pl.ds(pl.multiple_of(h * CH, CH), CH), 2 * CH * pair : 2 * CH * (pair + 1)] = (
                    result[:CH] + result[CH:]
                )
            return carry

        lax.fori_loop(0, piece_tiles, tile_step, 0)
        result = transform(total[...], tables, 1)
        directions[here(m), :] = result * lax.rsqrt(result * result + 0.04)

    def here(m):
        return pl.ds(pl.multiple_of(m * chunk, chunk), chunk)

    def own(m):
        q = z * pieces + m
        partial(q)

        @pl.when(z > 0)
        def _():
            add_arrived(q, 0, 1)

        @pl.when(z < lines - 1)
        def _():
            add_arrived(q, 1, -1)

        moment = 0.9 * mom[here(m), :] + acc[...].T
        coefficients = transform(moment, tables, 0)
        head, tail = split(coefficients)
        for h in range(piece_tiles):
            i = m * piece_tiles + h
            codes = lists[rep, i]
            picks = []
            for pair in range(pairs):
                at = (slice(h * CH, (h + 1) * CH), slice(2 * CH * pair, 2 * CH * (pair + 1)))
                cols = cols_hot[i, pair, :, pl.ds(pl.multiple_of(rep * span, span), span)]
                found = dot(jnp.concatenate([head[at], tail[at]], axis=0), cols)
                found = found[:CH] + found[CH:]
                row = row_codes(codes, pair)
                spots = lax.broadcasted_iota(jnp.int32, found.shape, 0)
                pick = jnp.sum(jnp.where(spots == row, found, 0.0), axis=0, keepdims=True)
                picks += [pick[:, : pick.shape[1] // 2], pick[:, pick.shape[1] // 2 :]]
            values[rep, i] = jnp.concatenate(picks, axis=0)
        for o in range(1, reps):
            value_copy(o, m).start()
        chosen = jnp.where(mask[here(m), :] > 0.5, coefficients, 0.0)
        mom[here(m), :] = moment - transform(chosen, tables, 1)

    def late_step(m, carry):
        for k in (plain + 2 * m + 1, plain + 2 * m + 2):
            line_step(k, 0)

        @pl.when(m > 0)
        def _():
            decode(m - 1)

        own(m)
        return carry

    lax.fori_loop(0, pieces, late_step, 0)
    decode(pieces - 1)

    for m in range(pieces):
        sib_copy(z * pieces + m).wait_send()

    def left_step(k, carry):
        def wait(q):
            sib_copy(q).wait_send()

        each(k, wait, wait)
        return carry

    lax.fori_loop(0, steps + 1, left_step, 0)
    for k in range(steps + 1 - DEPTH, steps + 1):
        each(k, sent(0, 1), sent(1, -1))


def body(lines, reps, activations, out_grads, momentum, indices, counts):
    inputs, grads, moment, places = activations[0], out_grads[0], momentum[0], indices[0]
    tokens, model = inputs.shape
    owned, width = moment.shape
    tile_cols, slots = places.shape[1:]
    chunk = 4 * CH
    fill = -owned % chunk
    rows = owned + fill
    if fill:
        inputs = inputs.reshape(tokens, 2 * lines, owned)
        inputs = jnp.pad(inputs, ((0, 0), (0, 0), (0, fill))).reshape(tokens, 2 * lines * rows)
        moment = jnp.pad(moment, ((0, fill), (0, 0)))
        places = jnp.pad(places, ((0, fill // CH), (0, 0), (0, 0)), constant_values=-1)
    tile_rows = rows // CH
    pieces = rows // chunk
    count = lines * pieces
    sizes = (lines, reps, rows, chunk, pieces, width, tokens)
    vmem = pl.BlockSpec(memory_space=pltpu.VMEM)
    hbm = pl.BlockSpec(memory_space=pltpu.HBM)
    dma = pltpu.SemaphoreType.DMA
    new_moment, step_dir = pl.pallas_call(
        functools.partial(kernel, sizes),
        out_shape=(
            pltpu.VMEM((rows, width), jnp.float32),
            pltpu.VMEM((rows, width), jnp.float32),
        ),
        in_specs=[vmem, hbm, hbm, hbm, vmem, hbm],
        out_specs=(vmem, vmem),
        scratch_shapes=[
            pltpu.VMEM((count, tokens, chunk), jnp.bfloat16),
            pltpu.VMEM((count, tokens, chunk), jnp.bfloat16),
            pltpu.VMEM((tokens, width), jnp.bfloat16),
            pltpu.VMEM((tokens, width), jnp.bfloat16),
            pltpu.VMEM((2, width, tokens), jnp.bfloat16),
            pltpu.VMEM((width, chunk), jnp.float32),
            pltpu.VMEM((count, width, chunk), jnp.int16),
            pltpu.VMEM((count, 1, chunk), jnp.float32),
            pltpu.VMEM((2, count, width, chunk), jnp.int16),
            pltpu.VMEM((2, count, 1, chunk), jnp.float32),
            pltpu.VMEM((reps, tile_rows, tile_cols, slots), jnp.int32),
            pltpu.VMEM((reps, tile_rows, tile_cols, slots), jnp.float32),
            pltpu.VMEM((rows, width), jnp.float32),
            pltpu.VMEM((tile_rows, tile_cols // 2, 2 * CH, reps * 2 * slots), jnp.bfloat16),
            pltpu.VMEM((chunk, width), jnp.float32),
            pltpu.VMEM((4, 4 * CH, 4 * CH), jnp.bfloat16),
            dma((count,)),
            dma((count,)),
            dma((count,)),
            dma((5,)),
            dma((2, count)),
            dma((2, 2, count)),
            dma((pieces + 1, reps)),
            dma((pieces + 1, reps)),
        ],
        compiler_params=pltpu.CompilerParams(
            collective_id=0, has_side_effects=True, vmem_limit_bytes=60 * 1024 * 1024 + 768 * 1024
        ),
        cost_estimate=pl.CostEstimate(
            flops=2 * tokens * model * width, bytes_accessed=2 * tokens * model, transcendentals=0
        ),
    )(counts.reshape(1, 1), inputs, grads, moment, places, jnp.asarray(cosine_tables()))
    return (new_moment[None, :owned], step_dir[:owned])


def solution(mesh):
    lines, reps = mesh.shape["fsdp"] // 2, mesh.shape["rep"]
    placed = (
        P("rep", "fsdp", None),
        P("rep", "fsdp", None),
        P("rep", "fsdp", None),
        P("rep", "fsdp", None, None),
        P("rep"),
    )
    return jax.shard_map(
        functools.partial(body, lines, reps),
        mesh=mesh,
        in_specs=placed,
        out_specs=(P("rep", "fsdp", None), P("fsdp", None)),
        check_vma=False,
    )
```

```python
import functools
import math

import jax
import jax.numpy as jnp
import numpy as np
from jax import lax
from jax.experimental import pallas as pl
from jax.experimental.pallas import tpu as pltpu
from jax.sharding import PartitionSpec as P
import ml_dtypes

CH = 64
MESH = pl.DeviceIdType.MESH
LEVELS = 32000.0
DEPTH = 6


def cosine_tables():
    freq = np.arange(CH, dtype=np.float64)[:, None]
    place = np.arange(CH, dtype=np.float64)[None, :]
    table = np.cos(math.pi * (2 * place + 1) * freq / (2 * CH)) * math.sqrt(2.0 / CH)
    table[0] *= math.sqrt(0.5)
    whole = np.kron(np.eye(4), table).astype(np.float32)
    head = whole.astype(ml_dtypes.bfloat16)
    tail = (whole - head.astype(np.float32)).astype(ml_dtypes.bfloat16)
    return np.stack([head.T, tail.T, head, tail])


def split(value):
    head = value.astype(jnp.bfloat16)
    return head, (value - head.astype(jnp.float32)).astype(jnp.bfloat16)


def dot(a, b, contract=((1,), (0,))):
    return lax.dot_general(a, b, (contract, ((), ())), preferred_element_type=jnp.float32)


def transform(field, tables, way):
    height, width = field.shape
    rh, rl = tables[2 * way], tables[2 * way + 1]
    other = 2 - 2 * way
    lh, ll = tables[other, :height, :height], tables[other + 1, :height, :height]
    stack = jnp.concatenate([lh, ll], axis=0)
    parts = []
    for start in range(0, width, 256):
        fh, fl = split(field[:, start : start + 256])
        both = dot(jnp.concatenate([fh, fl], axis=0), rh)
        yh, yl = split(both[:height] + (dot(fh, rl) + both[height:]))
        both = dot(stack, yh)
        parts.append(both[:height] + (dot(lh, yl) + both[height:]))
    return jnp.concatenate(parts, axis=1)


def pair_rows(rows, pair):
    a = rows[2 * pair : 2 * pair + 1, :]
    b = rows[2 * pair + 1 : 2 * pair + 2, :]
    return a, b


def row_codes(rows, pair):
    a, b = pair_rows(rows, pair)
    return jnp.concatenate([a >> 6, b >> 6], axis=1)


def column_hot(rows, pair):
    a, b = pair_rows(rows, pair)
    codes = jnp.concatenate([a & 63, (b & 63) + 64], axis=1)
    spots = lax.broadcasted_iota(jnp.int32, (2 * CH, codes.shape[1]), 0)
    return jnp.where(spots == codes, 1.0, 0.0).astype(jnp.bfloat16)


def kernel(
    sizes,
    counts_ref, act_hbm, grad_hbm, mom_hbm, places_ref, tables_hbm,
    mom, directions,
    own_act, sib_act, own_grad, sib_grad, flipped, acc, coded, scales, in_coded, in_scales,
    lists, values, mask, cols_hot, total, tables,
    act_sem, sib_send, sib_recv, misc_sem, out_send, out_recv, rep_send, rep_recv,
):
    lines, reps, rows, chunk, pieces, width, tokens = sizes
    pairs = width // CH // 2
    tile_rows = rows // CH
    piece_tiles = chunk // CH
    span = 2 * lists.shape[-1]
    f = lax.axis_index("fsdp")
    rep = lax.axis_index("rep")
    z, core = f // 2, f % 2
    sibling = {"fsdp": 2 * z + 1 - core}

    def along(step):
        return {"fsdp": 2 * (z + step) + core}

    grad_own = pltpu.make_async_copy(grad_hbm, own_grad, misc_sem.at[0])
    mom_own = pltpu.make_async_copy(mom_hbm, mom, misc_sem.at[1])
    tables_own = pltpu.make_async_copy(tables_hbm, tables, misc_sem.at[4])
    grad_own.start()

    barrier = pltpu.get_barrier_semaphore()
    pl.semaphore_signal(barrier, inc=1, device_id=sibling, device_id_type=MESH)

    @pl.when(z > 0)
    def _():
        pl.semaphore_signal(barrier, inc=1, device_id=along(-1), device_id_type=MESH)

    @pl.when(z < lines - 1)
    def _():
        pl.semaphore_signal(barrier, inc=1, device_id=along(1), device_id_type=MESH)

    for o in range(1, reps):
        pl.semaphore_signal(
            barrier, inc=1, device_id={"rep": lax.rem(rep + o, reps)}, device_id_type=MESH
        )

    used = lax.broadcasted_iota(jnp.int32, places_ref.shape[1:], 1) < counts_ref[...]
    for i in range(tile_rows):
        lists[rep, i] = jnp.where(used, places_ref[i], -1)

    def source(q, lane):
        start = (2 * (q // pieces) + lane) * rows + (q % pieces) * chunk
        return act_hbm.at[:, pl.ds(pl.multiple_of(start, 128), chunk)]

    def own_copy(q):
        return pltpu.make_async_copy(source(q, core), own_act.at[q], act_sem.at[q])

    def sib_copy(q):
        return pltpu.make_async_remote_copy(
            src_ref=source(q, 1 - core), dst_ref=sib_act.at[q],
            send_sem=sib_send.at[q], recv_sem=sib_recv.at[q],
            device_id=sibling, device_id_type=MESH,
        )

    grad_sib = pltpu.make_async_remote_copy(
        src_ref=grad_hbm, dst_ref=sib_grad, send_sem=misc_sem.at[2], recv_sem=misc_sem.at[3],
        device_id=sibling, device_id_type=MESH,
    )

    steps = (lines - 1) * pieces
    plain = (lines - 3) * pieces

    def owner(k):
        later = k - plain
        block = jnp.where(later < 0, lines - 1 - k // pieces, 2 - later % 2)
        piece = jnp.where(later < 0, k % pieces, later // 2)
        return block, piece

    def each(tick, right, left):
        k = tick - z
        block, piece = owner(k)

        @pl.when((k >= 0) & (k < steps) & (block > z))
        def _():
            right(block * pieces + piece)

        j = tick - (lines - 1 - z)
        facing, part = owner(j)

        @pl.when((j >= 0) & (j < steps) & (lines - 1 - facing < z))
        def _():
            left((lines - 1 - facing) * pieces + part)

    def fetch(q):
        own_copy(q).start()
        sib_copy(q).start()

    neighbours = 1 + jnp.where(z > 0, 1, 0) + jnp.where(z < lines - 1, 1, 0) + (reps - 1)
    pl.semaphore_wait(barrier, neighbours)
    grad_sib.start()
    each(0, fetch, fetch)

    def list_copy(o):
        return pltpu.make_async_remote_copy(
            src_ref=lists.at[rep], dst_ref=lists.at[rep],
            send_sem=rep_send.at[pieces, o], recv_sem=rep_recv.at[pieces, o],
            device_id={"rep": lax.rem(rep + o, reps)}, device_id_type=MESH,
        )

    def value_copy(o, m):
        part = values.at[rep, pl.ds(m * piece_tiles, piece_tiles)]
        return pltpu.make_async_remote_copy(
            src_ref=part, dst_ref=part,
            send_sem=rep_send.at[m, o], recv_sem=rep_recv.at[m, o],
            device_id={"rep": lax.rem(rep + o, reps)}, device_id_type=MESH,
        )

    grad_own.wait()
    flipped[0] = own_grad[...].T
    grad_sib.wait()
    flipped[1] = sib_grad[...].T
    each(1, fetch, fetch)
    each(2, fetch, fetch)
    for o in range(1, reps):
        list_copy(o).start()

    def partial(q):
        own_copy(q).wait()
        sib_copy(q).wait_recv()
        acc[...] = dot(flipped[0], own_act[q]) + dot(flipped[1], sib_act[q])

    def chunk_copies(q, way, step):
        return [
            pltpu.make_async_remote_copy(
                src_ref=src.at[q], dst_ref=dst.at[way, q],
                send_sem=out_send.at[kind, q], recv_sem=out_recv.at[kind, way, q],
                device_id=along(step), device_id_type=MESH,
            )
            for kind, (src, dst) in enumerate(((coded, in_coded), (scales, in_scales)))
        ]

    def add_arrived(q, way, step):
        for copy in chunk_copies(q, way, step):
            copy.wait_recv()
        acc[...] += in_coded[way, q].astype(jnp.int32).astype(jnp.float32) * in_scales[way, q]

    def pass_on(q, way, step):
        value = acc[...]
        top = jnp.maximum(jnp.max(jnp.abs(value), axis=0, keepdims=True), 1e-30)
        scales[q] = top * (1.0 / LEVELS)
        coded[q] = jnp.round(value * (LEVELS / top)).astype(jnp.int32).astype(jnp.int16)
        for copy in chunk_copies(q, way, step):
            copy.start()

    def right(q):
        partial(q)

        @pl.when(z > 0)
        def _():
            add_arrived(q, 0, 1)

        pass_on(q, 0, 1)

    def left(q):
        partial(q)

        @pl.when(z < lines - 1)
        def _():
            add_arrived(q, 1, -1)

        pass_on(q, 1, -1)

    def sent(way, step):
        def wait(q):
            for copy in chunk_copies(q, way, step):
                copy.wait_send()

        return wait

    def line_step(k, carry):
        each(k - DEPTH, sent(0, 1), sent(1, -1))

        each(k + 3, fetch, fetch)

        @pl.when(k < pieces)
        def _():
            fetch(z * pieces + k)

        each(k, right, left)
        return carry

    def mask_step(i, carry):
        codes = lists[rep, i]
        for pair in range(pairs):
            row = row_codes(codes, pair)
            spots = lax.broadcasted_iota(jnp.int32, (CH, row.shape[1]), 0)
            hot = jnp.where(spots == row, 1.0, 0.0).astype(jnp.bfloat16)
            cols = column_hot(codes, pair)
            mask[pl.ds(pl.multiple_of(i * CH, CH), CH), 2 * CH * pair : 2 * CH * (pair + 1)] = (
                dot(hot, cols, ((1,), (1,)))
            )
        return carry

    def hot_step(n, carry):
        for r in range(reps):
            for pair in range(pairs):
                cols_hot[n, pair, :, r * span : (r + 1) * span] = column_hot(lists[r, n], pair)
        return carry

    def prepare():
        mom_own.start()
        tables_own.start()
        lax.fori_loop(0, tile_rows, mask_step, 0)
        for o in range(1, reps):
            list_copy(o).wait()
        lax.fori_loop(0, tile_rows, hot_step, 0)
        mom_own.wait()
        tables_own.wait()

    middle = (z > 0) & (z < lines - 1)

    @pl.when(middle)
    def _():
        prepare()

    line_step(0, 0)

    @pl.when(jnp.logical_not(middle))
    def _():
        prepare()

    lax.fori_loop(1, plain + 1, line_step, 0)

    def decode(m):
        for o in range(1, reps):
            value_copy(o, m).wait()

        def tile_step(h, carry):
            i = m * piece_tiles + h
            for pair in range(pairs):
                parts = []
                for r in range(reps):
                    row = row_codes(lists[r, i], pair)
                    a, b = pair_rows(values[r, i], pair)
                    head, tail = split(jnp.concatenate([a, b], axis=1))
                    spots = lax.broadcasted_iota(jnp.int32, (CH, row.shape[1]), 0)
                    hit = spots == row
                    both = jnp.concatenate(
                        [
                            jnp.where(hit, head.astype(jnp.float32), 0.0),
                            jnp.where(hit, tail.astype(jnp.float32), 0.0),
                        ],
                        axis=0,
                    ).astype(jnp.bfloat16)
                    parts.append(both)
                result = dot(jnp.concatenate(parts, axis=1), cols_hot[i, pair], ((1,), (1,)))
                total[pl.ds(pl.multiple_of(h * CH, CH), CH), 2 * CH * pair : 2 * CH * (pair + 1)] = (
                    result[:CH] + result[CH:]
                )
            return carry

        lax.fori_loop(0, piece_tiles, tile_step, 0)
        result = transform(total[...], tables, 1)
        directions[here(m), :] = result * lax.rsqrt(result * result + 0.04)

    def here(m):
        return pl.ds(pl.multiple_of(m * chunk, chunk), chunk)

    def own(m):
        q = z * pieces + m
        partial(q)

        @pl.when(z > 0)
        def _():
            add_arrived(q, 0, 1)

        @pl.when(z < lines - 1)
        def _():
            add_arrived(q, 1, -1)

        moment = 0.9 * mom[here(m), :] + acc[...].T
        coefficients = transform(moment, tables, 0)
        head, tail = split(coefficients)
        for h in range(piece_tiles):
            i = m * piece_tiles + h
            codes = lists[rep, i]
            picks = []
            for pair in range(pairs):
                at = (slice(h * CH, (h + 1) * CH), slice(2 * CH * pair, 2 * CH * (pair + 1)))
                cols = cols_hot[i, pair, :, pl.ds(pl.multiple_of(rep * span, span), span)]
                found = dot(jnp.concatenate([head[at], tail[at]], axis=0), cols)
                found = found[:CH] + found[CH:]
                row = row_codes(codes, pair)
                spots = lax.broadcasted_iota(jnp.int32, found.shape, 0)
                pick = jnp.sum(jnp.where(spots == row, found, 0.0), axis=0, keepdims=True)
                picks += [pick[:, : pick.shape[1] // 2], pick[:, pick.shape[1] // 2 :]]
            values[rep, i] = jnp.concatenate(picks, axis=0)
        for o in range(1, reps):
            value_copy(o, m).start()
        chosen = jnp.where(mask[here(m), :] > 0.5, coefficients, 0.0)
        mom[here(m), :] = moment - transform(chosen, tables, 1)

    def late_step(m, carry):
        for k in (plain + 2 * m + 1, plain + 2 * m + 2):
            line_step(k, 0)

        @pl.when(m > 0)
        def _():
            decode(m - 1)

        own(m)
        return carry

    lax.fori_loop(0, pieces, late_step, 0)
    decode(pieces - 1)

    for m in range(pieces):
        sib_copy(z * pieces + m).wait_send()

    def left_step(k, carry):
        def wait(q):
            sib_copy(q).wait_send()

        each(k, wait, wait)
        return carry

    lax.fori_loop(0, steps + 1, left_step, 0)
    for k in range(steps + 1 - DEPTH, steps + 1):
        each(k, sent(0, 1), sent(1, -1))


def body(lines, reps, activations, out_grads, momentum, indices, counts):
    inputs, grads, moment, places = activations[0], out_grads[0], momentum[0], indices[0]
    tokens, model = inputs.shape
    owned, width = moment.shape
    tile_cols, slots = places.shape[1:]
    chunk = 2 * CH
    fill = -owned % chunk
    rows = owned + fill
    if fill:
        inputs = inputs.reshape(tokens, 2 * lines, owned)
        inputs = jnp.pad(inputs, ((0, 0), (0, 0), (0, fill))).reshape(tokens, 2 * lines * rows)
        moment = jnp.pad(moment, ((0, fill), (0, 0)))
        places = jnp.pad(places, ((0, fill // CH), (0, 0), (0, 0)), constant_values=-1)
    tile_rows = rows // CH
    pieces = rows // chunk
    count = lines * pieces
    sizes = (lines, reps, rows, chunk, pieces, width, tokens)
    vmem = pl.BlockSpec(memory_space=pltpu.VMEM)
    hbm = pl.BlockSpec(memory_space=pltpu.HBM)
    dma = pltpu.SemaphoreType.DMA
    new_moment, step_dir = pl.pallas_call(
        functools.partial(kernel, sizes),
        out_shape=(
            pltpu.VMEM((rows, width), jnp.float32),
            pltpu.VMEM((rows, width), jnp.float32),
        ),
        in_specs=[vmem, hbm, hbm, hbm, vmem, hbm],
        out_specs=(vmem, vmem),
        scratch_shapes=[
            pltpu.VMEM((count, tokens, chunk), jnp.bfloat16),
            pltpu.VMEM((count, tokens, chunk), jnp.bfloat16),
            pltpu.VMEM((tokens, width), jnp.bfloat16),
            pltpu.VMEM((tokens, width), jnp.bfloat16),
            pltpu.VMEM((2, width, tokens), jnp.bfloat16),
            pltpu.VMEM((width, chunk), jnp.float32),
            pltpu.VMEM((count, width, chunk), jnp.int16),
            pltpu.VMEM((count, 1, chunk), jnp.float32),
            pltpu.VMEM((2, count, width, chunk), jnp.int16),
            pltpu.VMEM((2, count, 1, chunk), jnp.float32),
            pltpu.VMEM((reps, tile_rows, tile_cols, slots), jnp.int32),
            pltpu.VMEM((reps, tile_rows, tile_cols, slots), jnp.float32),
            pltpu.VMEM((rows, width), jnp.float32),
            pltpu.VMEM((tile_rows, tile_cols // 2, 2 * CH, reps * 2 * slots), jnp.bfloat16),
            pltpu.VMEM((chunk, width), jnp.float32),
            pltpu.VMEM((4, 4 * CH, 4 * CH), jnp.bfloat16),
            dma((count,)),
            dma((count,)),
            dma((count,)),
            dma((5,)),
            dma((2, count)),
            dma((2, 2, count)),
            dma((pieces + 1, reps)),
            dma((pieces + 1, reps)),
        ],
        compiler_params=pltpu.CompilerParams(
            collective_id=0, has_side_effects=True, vmem_limit_bytes=60 * 1024 * 1024 + 768 * 1024
        ),
        cost_estimate=pl.CostEstimate(
            flops=2 * tokens * model * width, bytes_accessed=2 * tokens * model, transcendentals=0
        ),
    )(counts.reshape(1, 1), inputs, grads, moment, places, jnp.asarray(cosine_tables()))
    return (new_moment[None, :owned], step_dir[:owned])


def solution(mesh):
    lines, reps = mesh.shape["fsdp"] // 2, mesh.shape["rep"]
    placed = (
        P("rep", "fsdp", None),
        P("rep", "fsdp", None),
        P("rep", "fsdp", None),
        P("rep", "fsdp", None, None),
        P("rep"),
    )
    return jax.shard_map(
        functools.partial(body, lines, reps),
        mesh=mesh,
        in_specs=placed,
        out_specs=(P("rep", "fsdp", None), P("fsdp", None)),
        check_vma=False,
    )
```

```python
import functools
import math

import jax
import jax.numpy as jnp
import numpy as np
from jax import lax
from jax.experimental import pallas as pl
from jax.experimental.pallas import tpu as pltpu
from jax.sharding import PartitionSpec as P
import ml_dtypes

CH = 64
MESH = pl.DeviceIdType.MESH
LEVELS = 32000.0
DEPTH = 3


def cosine_tables():
    freq = np.arange(CH, dtype=np.float64)[:, None]
    place = np.arange(CH, dtype=np.float64)[None, :]
    table = np.cos(math.pi * (2 * place + 1) * freq / (2 * CH)) * math.sqrt(2.0 / CH)
    table[0] *= math.sqrt(0.5)
    whole = np.kron(np.eye(4), table).astype(np.float32)
    head = whole.astype(ml_dtypes.bfloat16)
    tail = (whole - head.astype(np.float32)).astype(ml_dtypes.bfloat16)
    return np.stack([head.T, tail.T, head, tail])


def split(value):
    head = value.astype(jnp.bfloat16)
    return head, (value - head.astype(jnp.float32)).astype(jnp.bfloat16)


def dot(a, b, contract=((1,), (0,))):
    return lax.dot_general(a, b, (contract, ((), ())), preferred_element_type=jnp.float32)


def transform(field, tables, way):
    height, width = field.shape
    rh, rl = tables[2 * way], tables[2 * way + 1]
    other = 2 - 2 * way
    lh, ll = tables[other, :height, :height], tables[other + 1, :height, :height]
    stack = jnp.concatenate([lh, ll], axis=0)
    parts = []
    for start in range(0, width, 256):
        fh, fl = split(field[:, start : start + 256])
        both = dot(jnp.concatenate([fh, fl], axis=0), rh)
        yh, yl = split(both[:height] + (dot(fh, rl) + both[height:]))
        both = dot(stack, yh)
        parts.append(both[:height] + (dot(lh, yl) + both[height:]))
    return jnp.concatenate(parts, axis=1)


def pair_rows(rows, pair):
    a = rows[2 * pair : 2 * pair + 1, :]
    b = rows[2 * pair + 1 : 2 * pair + 2, :]
    return a, b


def row_codes(rows, pair):
    a, b = pair_rows(rows, pair)
    return jnp.concatenate([a >> 6, b >> 6], axis=1)


def column_hot(rows, pair):
    a, b = pair_rows(rows, pair)
    codes = jnp.concatenate([a & 63, (b & 63) + 64], axis=1)
    spots = lax.broadcasted_iota(jnp.int32, (2 * CH, codes.shape[1]), 0)
    return jnp.where(spots == codes, 1.0, 0.0).astype(jnp.bfloat16)


def kernel(
    sizes,
    counts_ref, act_hbm, grad_hbm, mom_hbm, places_ref, tables_hbm,
    mom, directions,
    acts, own_grad, sib_grad, flipped, acc, coded, scales, in_coded, in_scales,
    lists, values, mask, cols_hot, total, tables,
    act_sem, sib_send, sib_recv, misc_sem, out_send, out_recv, rep_send, rep_recv,
):
    lines, reps, rows, chunk, pieces, width, tokens = sizes
    pairs = width // CH // 2
    tile_rows = rows // CH
    piece_tiles = chunk // CH
    span = 2 * lists.shape[-1]
    f = lax.axis_index("fsdp")
    rep = lax.axis_index("rep")
    z, core = f // 2, f % 2
    sibling = {"fsdp": 2 * z + 1 - core}

    def along(step):
        return {"fsdp": 2 * (z + step) + core}

    grad_own = pltpu.make_async_copy(grad_hbm, own_grad, misc_sem.at[0])
    mom_own = pltpu.make_async_copy(mom_hbm, mom, misc_sem.at[1])
    tables_own = pltpu.make_async_copy(tables_hbm, tables, misc_sem.at[4])
    grad_own.start()

    barrier = pltpu.get_barrier_semaphore()
    pl.semaphore_signal(barrier, inc=1, device_id=sibling, device_id_type=MESH)

    @pl.when(z > 0)
    def _():
        pl.semaphore_signal(barrier, inc=1, device_id=along(-1), device_id_type=MESH)

    @pl.when(z < lines - 1)
    def _():
        pl.semaphore_signal(barrier, inc=1, device_id=along(1), device_id_type=MESH)

    for o in range(1, reps):
        pl.semaphore_signal(
            barrier, inc=1, device_id={"rep": lax.rem(rep + o, reps)}, device_id_type=MESH
        )

    used = lax.broadcasted_iota(jnp.int32, places_ref.shape[1:], 1) < counts_ref[...]
    for i in range(tile_rows):
        lists[rep, i] = jnp.where(used, places_ref[i], -1)

    def source(q, lane):
        start = (2 * (q // pieces) + lane) * rows + (q % pieces) * chunk
        return act_hbm.at[:, pl.ds(pl.multiple_of(start, 128), chunk)]

    def own_copy(q):
        return pltpu.make_async_copy(source(q, core), acts.at[q, pl.ds(0, tokens)], act_sem.at[q])

    def sib_copy(q):
        return pltpu.make_async_remote_copy(
            src_ref=source(q, 1 - core), dst_ref=acts.at[q, pl.ds(tokens, tokens)],
            send_sem=sib_send.at[q], recv_sem=sib_recv.at[q],
            device_id=sibling, device_id_type=MESH,
        )

    grad_sib = pltpu.make_async_remote_copy(
        src_ref=grad_hbm, dst_ref=sib_grad, send_sem=misc_sem.at[2], recv_sem=misc_sem.at[3],
        device_id=sibling, device_id_type=MESH,
    )

    steps = (lines - 1) * pieces
    plain = (lines - 3) * pieces

    def owner(k):
        later = k - plain
        block = jnp.where(later < 0, lines - 1 - k // pieces, 2 - later % 2)
        piece = jnp.where(later < 0, k % pieces, later // 2)
        return block, piece

    def each(tick, right, left):
        k = tick - z
        block, piece = owner(k)

        @pl.when((k >= 0) & (k < steps) & (block > z))
        def _():
            right(block * pieces + piece)

        j = tick - (lines - 1 - z)
        facing, part = owner(j)

        @pl.when((j >= 0) & (j < steps) & (lines - 1 - facing < z))
        def _():
            left((lines - 1 - facing) * pieces + part)

    def fetch(q):
        own_copy(q).start()
        sib_copy(q).start()

    neighbours = 1 + jnp.where(z > 0, 1, 0) + jnp.where(z < lines - 1, 1, 0) + (reps - 1)
    pl.semaphore_wait(barrier, neighbours)
    grad_sib.start()
    each(0, fetch, fetch)

    def list_copy(o):
        return pltpu.make_async_remote_copy(
            src_ref=lists.at[rep], dst_ref=lists.at[rep],
            send_sem=rep_send.at[pieces, o], recv_sem=rep_recv.at[pieces, o],
            device_id={"rep": lax.rem(rep + o, reps)}, device_id_type=MESH,
        )

    def value_copy(o, m):
        part = values.at[rep, pl.ds(m * piece_tiles, piece_tiles)]
        return pltpu.make_async_remote_copy(
            src_ref=part, dst_ref=part,
            send_sem=rep_send.at[m, o], recv_sem=rep_recv.at[m, o],
            device_id={"rep": lax.rem(rep + o, reps)}, device_id_type=MESH,
        )

    grad_own.wait()
    flipped[:, :tokens] = own_grad[...].T
    grad_sib.wait()
    flipped[:, tokens:] = sib_grad[...].T
    each(1, fetch, fetch)
    for o in range(1, reps):
        list_copy(o).start()

    def partial(q):
        own_copy(q).wait()
        sib_copy(q).wait_recv()
        acc[...] = dot(flipped[...], acts[q])

    def chunk_copies(q, way, step):
        return [
            pltpu.make_async_remote_copy(
                src_ref=src.at[q], dst_ref=dst.at[way, q],
                send_sem=out_send.at[kind, q], recv_sem=out_recv.at[kind, way, q],
                device_id=along(step), device_id_type=MESH,
            )
            for kind, (src, dst) in enumerate(((coded, in_coded), (scales, in_scales)))
        ]

    def add_arrived(q, way, step):
        for copy in chunk_copies(q, way, step):
            copy.wait_recv()
        acc[...] += in_coded[way, q].astype(jnp.int32).astype(jnp.float32) * in_scales[way, q]

    def pass_on(q, way, step):
        value = acc[...]
        top = jnp.maximum(jnp.max(jnp.abs(value), axis=0, keepdims=True), 1e-30)
        scales[q] = top * (1.0 / LEVELS)
        coded[q] = jnp.round(value * (LEVELS / top)).astype(jnp.int32).astype(jnp.int16)
        for copy in chunk_copies(q, way, step):
            copy.start()

    def right(q):
        partial(q)

        @pl.when(z > 0)
        def _():
            add_arrived(q, 0, 1)

        pass_on(q, 0, 1)

    def left(q):
        partial(q)

        @pl.when(z < lines - 1)
        def _():
            add_arrived(q, 1, -1)

        pass_on(q, 1, -1)

    def sent(way, step):
        def wait(q):
            for copy in chunk_copies(q, way, step):
                copy.wait_send()

        return wait

    def line_step(k, carry):
        each(k - DEPTH, sent(0, 1), sent(1, -1))

        each(k + 2, fetch, fetch)

        @pl.when(k < pieces)
        def _():
            fetch(z * pieces + k)

        each(k, right, left)
        return carry

    def mask_step(i, carry):
        codes = lists[rep, i]
        for pair in range(pairs):
            row = row_codes(codes, pair)
            spots = lax.broadcasted_iota(jnp.int32, (CH, row.shape[1]), 0)
            hot = jnp.where(spots == row, 1.0, 0.0).astype(jnp.bfloat16)
            cols = column_hot(codes, pair)
            mask[pl.ds(pl.multiple_of(i * CH, CH), CH), 2 * CH * pair : 2 * CH * (pair + 1)] = (
                dot(hot, cols, ((1,), (1,)))
            )
        return carry

    def hot_step(n, carry):
        for r in range(reps):
            for pair in range(pairs):
                cols_hot[n, pair, :, r * span : (r + 1) * span] = column_hot(lists[r, n], pair)
        return carry

    def prepare():
        mom_own.start()
        tables_own.start()
        lax.fori_loop(0, tile_rows, mask_step, 0)
        for o in range(1, reps):
            list_copy(o).wait()
        lax.fori_loop(0, tile_rows, hot_step, 0)
        mom_own.wait()
        tables_own.wait()

    middle = (z > 0) & (z < lines - 1)

    @pl.when(middle)
    def _():
        prepare()

    line_step(0, 0)

    @pl.when(jnp.logical_not(middle))
    def _():
        prepare()

    lax.fori_loop(1, plain + 1, line_step, 0)

    def decode(m):
        for o in range(1, reps):
            value_copy(o, m).wait()

        def tile_step(h, carry):
            i = m * piece_tiles + h
            for pair in range(pairs):
                parts = []
                for r in range(reps):
                    row = row_codes(lists[r, i], pair)
                    a, b = pair_rows(values[r, i], pair)
                    head, tail = split(jnp.concatenate([a, b], axis=1))
                    spots = lax.broadcasted_iota(jnp.int32, (CH, row.shape[1]), 0)
                    hit = spots == row
                    both = jnp.concatenate(
                        [
                            jnp.where(hit, head.astype(jnp.float32), 0.0),
                            jnp.where(hit, tail.astype(jnp.float32), 0.0),
                        ],
                        axis=0,
                    ).astype(jnp.bfloat16)
                    parts.append(both)
                result = dot(jnp.concatenate(parts, axis=1), cols_hot[i, pair], ((1,), (1,)))
                total[pl.ds(pl.multiple_of(h * CH, CH), CH), 2 * CH * pair : 2 * CH * (pair + 1)] = (
                    result[:CH] + result[CH:]
                )
            return carry

        lax.fori_loop(0, piece_tiles, tile_step, 0)
        result = transform(total[...], tables, 1)
        directions[here(m), :] = result * lax.rsqrt(result * result + 0.04)

    def here(m):
        return pl.ds(pl.multiple_of(m * chunk, chunk), chunk)

    def own(m):
        q = z * pieces + m
        partial(q)

        @pl.when(z > 0)
        def _():
            add_arrived(q, 0, 1)

        @pl.when(z < lines - 1)
        def _():
            add_arrived(q, 1, -1)

        moment = 0.9 * mom[here(m), :] + acc[...].T
        coefficients = transform(moment, tables, 0)
        head, tail = split(coefficients)
        for h in range(piece_tiles):
            i = m * piece_tiles + h
            codes = lists[rep, i]
            picks = []
            for pair in range(pairs):
                at = (slice(h * CH, (h + 1) * CH), slice(2 * CH * pair, 2 * CH * (pair + 1)))
                cols = cols_hot[i, pair, :, pl.ds(pl.multiple_of(rep * span, span), span)]
                found = dot(jnp.concatenate([head[at], tail[at]], axis=0), cols)
                found = found[:CH] + found[CH:]
                row = row_codes(codes, pair)
                spots = lax.broadcasted_iota(jnp.int32, found.shape, 0)
                pick = jnp.sum(jnp.where(spots == row, found, 0.0), axis=0, keepdims=True)
                picks += [pick[:, : pick.shape[1] // 2], pick[:, pick.shape[1] // 2 :]]
            values[rep, i] = jnp.concatenate(picks, axis=0)
        for o in range(1, reps):
            value_copy(o, m).start()
        chosen = jnp.where(mask[here(m), :] > 0.5, coefficients, 0.0)
        mom[here(m), :] = moment - transform(chosen, tables, 1)

    def late_step(m, carry):
        for k in (plain + 2 * m + 1, plain + 2 * m + 2):
            line_step(k, 0)

        @pl.when(m > 0)
        def _():
            decode(m - 1)

        own(m)
        return carry

    lax.fori_loop(0, pieces, late_step, 0)
    decode(pieces - 1)

    for m in range(pieces):
        sib_copy(z * pieces + m).wait_send()

    def left_step(k, carry):
        def wait(q):
            sib_copy(q).wait_send()

        each(k, wait, wait)
        return carry

    lax.fori_loop(0, steps + 1, left_step, 0)
    for k in range(steps + 1 - DEPTH, steps + 1):
        each(k, sent(0, 1), sent(1, -1))


def body(lines, reps, activations, out_grads, momentum, indices, counts):
    inputs, grads, moment, places = activations[0], out_grads[0], momentum[0], indices[0]
    tokens, model = inputs.shape
    owned, width = moment.shape
    tile_cols, slots = places.shape[1:]
    chunk = 4 * CH
    fill = -owned % chunk
    rows = owned + fill
    if fill:
        inputs = inputs.reshape(tokens, 2 * lines, owned)
        inputs = jnp.pad(inputs, ((0, 0), (0, 0), (0, fill))).reshape(tokens, 2 * lines * rows)
        moment = jnp.pad(moment, ((0, fill), (0, 0)))
        places = jnp.pad(places, ((0, fill // CH), (0, 0), (0, 0)), constant_values=-1)
    tile_rows = rows // CH
    pieces = rows // chunk
    count = lines * pieces
    sizes = (lines, reps, rows, chunk, pieces, width, tokens)
    vmem = pl.BlockSpec(memory_space=pltpu.VMEM)
    hbm = pl.BlockSpec(memory_space=pltpu.HBM)
    dma = pltpu.SemaphoreType.DMA
    new_moment, step_dir = pl.pallas_call(
        functools.partial(kernel, sizes),
        out_shape=(
            pltpu.VMEM((rows, width), jnp.float32),
            pltpu.VMEM((rows, width), jnp.float32),
        ),
        in_specs=[vmem, hbm, hbm, hbm, vmem, hbm],
        out_specs=(vmem, vmem),
        scratch_shapes=[
            pltpu.VMEM((count, 2 * tokens, chunk), jnp.bfloat16),
            pltpu.VMEM((tokens, width), jnp.bfloat16),
            pltpu.VMEM((tokens, width), jnp.bfloat16),
            pltpu.VMEM((width, 2 * tokens), jnp.bfloat16),
            pltpu.VMEM((width, chunk), jnp.float32),
            pltpu.VMEM((count, width, chunk), jnp.int16),
            pltpu.VMEM((count, 1, chunk), jnp.float32),
            pltpu.VMEM((2, count, width, chunk), jnp.int16),
            pltpu.VMEM((2, count, 1, chunk), jnp.float32),
            pltpu.VMEM((reps, tile_rows, tile_cols, slots), jnp.int32),
            pltpu.VMEM((reps, tile_rows, tile_cols, slots), jnp.float32),
            pltpu.VMEM((rows, width), jnp.float32),
            pltpu.VMEM((tile_rows, tile_cols // 2, 2 * CH, reps * 2 * slots), jnp.bfloat16),
            pltpu.VMEM((chunk, width), jnp.float32),
            pltpu.VMEM((4, 4 * CH, 4 * CH), jnp.bfloat16),
            dma((count,)),
            dma((count,)),
            dma((count,)),
            dma((5,)),
            dma((2, count)),
            dma((2, 2, count)),
            dma((pieces + 1, reps)),
            dma((pieces + 1, reps)),
        ],
        compiler_params=pltpu.CompilerParams(
            collective_id=0, has_side_effects=True, vmem_limit_bytes=60 * 1024 * 1024 + 768 * 1024
        ),
        cost_estimate=pl.CostEstimate(
            flops=2 * tokens * model * width, bytes_accessed=2 * tokens * model, transcendentals=0
        ),
    )(counts.reshape(1, 1), inputs, grads, moment, places, jnp.asarray(cosine_tables()))
    return (new_moment[None, :owned], step_dir[:owned])


def solution(mesh):
    lines, reps = mesh.shape["fsdp"] // 2, mesh.shape["rep"]
    placed = (
        P("rep", "fsdp", None),
        P("rep", "fsdp", None),
        P("rep", "fsdp", None),
        P("rep", "fsdp", None, None),
        P("rep"),
    )
    return jax.shard_map(
        functools.partial(body, lines, reps),
        mesh=mesh,
        in_specs=placed,
        out_specs=(P("rep", "fsdp", None), P("fsdp", None)),
        check_vma=False,
    )
```
